32 devices in a mesh: groups: 2 (over y), dp: 16 (over z, x, core).
Axes of the slice: x: 2, y: 2, z: 4, core: 2. Of those that a mesh axis runs over, the one named last changes fastest.
Arguments:
- tokens: bfloat16 [64, 8192], P(('groups', 'dp')), parts along dimension 0, may hold values from -6 to 6
- cotangent: bfloat16 [64, 8192], P(('groups', 'dp')), parts along dimension 0, may hold values from -6 to 6
- gate_weight: bfloat16 [8192, 16384], P(None, 'dp'), may hold values from -0.0625 to 0.0625
- up_weight: bfloat16 [8192, 16384], P(None, 'dp'), may hold values from -0.0625 to 0.0625
- down_weight: bfloat16 [16384, 8192], P('dp'), may hold values from -0.046875 to 0.046875
- kept_blocks: int32 [6, 128, 4], P('groups', 'dp'), parts along dimension 0, may hold values from 0 to 63, as said below
- kept_counts: int32 [6, 128], P('groups', 'dp'), parts along dimension 0, may hold values from 1 to 4, as said below
- sparse_delta: float32 [6, 128, 4, 128, 128], P('groups', 'dp'), parts along dimension 0, may hold values from -0.3125 to 0.3125
- first_moment: float32 [6, 128, 4, 128, 128], P('groups', 'dp'), parts along dimension 0, may hold values from -6 to 6
- second_moment: float32 [6, 128, 4, 128, 128], P('groups', 'dp'), parts along dimension 0, may hold values from 1 to 64
Outputs:
- input_grad: bfloat16 [64, 8192], P(('groups', 'dp')), parts along dimension 0
- new_delta: float32 [6, 128, 4, 128, 128], P('groups', 'dp'), parts along dimension 0
- new_first: float32 [6, 128, 4, 128, 128], P('groups', 'dp'), parts along dimension 0
- new_second: float32 [6, 128, 4, 128, 128], P('groups', 'dp'), parts along dimension 0
The draws below stay inside these ranges and needn't reach their ends.
There are 2 independent parts, one for each index of `groups`. The reference program is written for one: setup_inputs(seed, part) draws one part's arguments, and reference() takes and returns one part's arrays. A program takes and returns all parts, laid end to end along the dimension named above; an argument that names none is the same for every part. Nothing has to cross between parts.
Inputs may be any that keep to these rules, and one draw needn't show every extreme that they name: `kept_blocks`: within a tile the 4 positions are distinct, from 0 to 63; slots at or beyond the tile's count are ignored. `kept_counts`: some tile of every matrix has all 4 slots live.
All inputs are finite; a program needn't handle non-finite values.
Results may differ from the reference program's by a relative error of at most 0.0054.
Values may be sent and summed in bfloat16 or wider, within the bound.
No kernel may reach another device: no remote copies, remote signals or barrier semaphores. Data moves between devices by JAX's collectives and lax.ppermute only.
A program may use at most 320 MiB of HBM per device.

```python
import math
import jax
import jax.numpy as jnp
from jax import lax

D = 8192
FF = 16384
BLK = 128
KMAX = 4
TOKENS = 32
TILES = 128


def draw_kept_blocks(key, part):
    key = jax.random.fold_in(key, 11)
    nblk = D // BLK
    tiles = FF // BLK
    scores = jax.random.randint(key, (3, tiles, nblk), 0, 2 ** 20) * nblk + jnp.arange(nblk, dtype=jnp.int32)
    picked = lax.top_k(scores, KMAX)[1]
    return picked.astype(jnp.int32)


def draw_kept_counts(key, part):
    key = jax.random.fold_in(key, 12)
    first_key, second_key = jax.random.split(key)
    tiles = FF // BLK
    table = jnp.minimum(jnp.array([1, 1, 1, 1, 2, 2, 3, 4], dtype=jnp.int32), KMAX)
    picks = jax.random.randint(first_key, (3, tiles), 0, 8)
    counts = jnp.sum(jnp.where(picks[:, :, None] == jnp.arange(8, dtype=jnp.int32), table, 0), axis=-1)
    where_full = jax.random.randint(second_key, (3,), 0, tiles)
    counts = jnp.where(jnp.arange(tiles, dtype=jnp.int32)[None, :] == where_full[:, None], KMAX, counts)
    return counts.astype(jnp.int32)


def block_scale(stream_key, dims, cuts, low, top_value):
    factor_of = 1.0
    for dim, blocks in cuts:
        steps = jax.random.uniform(jax.random.fold_in(jax.random.fold_in(stream_key, 6), dim), (blocks,), jnp.float32, low / len(cuts), top_value / len(cuts))
        factor_of = factor_of * jnp.repeat(jnp.exp(steps), dims[dim] // blocks).reshape((-1,) + (1,) * (len(dims) - 1 - dim))
    return factor_of


def normal_values(key, extent, width, limit, shards=(), kind=jnp.bfloat16):
    result = width * jax.random.normal(key, extent, jnp.float32)
    if shards:
        result = result * block_scale(key, extent, shards, -0.22, 0.18)
    return jnp.clip(result, -limit, limit).astype(kind)


def setup_inputs(seed: int = 0, part: int = 0) -> dict:
    seeds = jax.random.split(jax.random.key(seed), 11)
    part_keys = jax.random.split(jax.random.fold_in(seeds[10], part), 11)
    return {
        "tokens": normal_values(part_keys[0], (TOKENS, D), 1.0, 6.0, ((0, 16),)),
        "cotangent": normal_values(part_keys[1], (TOKENS, D), 1.0, 6.0, ((0, 16),)),
        "gate_weight": normal_values(seeds[2], (D, FF), D ** -0.5, 0.0625, ((1, 16),)),
        "up_weight": normal_values(seeds[3], (D, FF), D ** -0.5, 0.0625, ((1, 16),)),
        "down_weight": normal_values(seeds[4], (FF, D), FF ** -0.5, 0.046875, ((0, 16),)),
        "kept_blocks": draw_kept_blocks(jax.random.fold_in(jax.random.fold_in(seeds[10], part), 71), part),
        "kept_counts": draw_kept_counts(jax.random.fold_in(jax.random.fold_in(seeds[10], part), 71), part),
        "sparse_delta": normal_values(part_keys[7], (3, TILES, KMAX, BLK, BLK), 0.02, 0.3125, ((1, 16),), jnp.float32),
        "first_moment": normal_values(part_keys[8], (3, TILES, KMAX, BLK, BLK), 1.0, 6.0, ((1, 16),), jnp.float32),
        "second_moment": jnp.clip(jnp.exp(math.log(64.0) - 4.158883 * jax.random.uniform(part_keys[9], (3, TILES, KMAX, BLK, BLK), jnp.float32) ** block_scale(part_keys[9], (3, TILES, KMAX, BLK, BLK), ((1, 16),), -0.2, 0.2)), 1.0, 64.0),
    }


def patch_columns(base, sparse, ids, live):
    nblk = base.shape[0] // BLK
    tiles = base.shape[1] // BLK
    grid = jnp.zeros((nblk, tiles, BLK, BLK), jnp.float32)
    tile_ids = jnp.broadcast_to(jnp.arange(tiles, dtype=jnp.int32)[:, None], ids.shape)
    grid = grid.at[ids, tile_ids].add(sparse * live[:, :, None, None])
    full = grid.transpose(0, 2, 1, 3).reshape(base.shape)
    return (base.astype(jnp.float32) + full).astype(jnp.bfloat16)

def patch_rows(base, sparse, ids, live):
    tiles = base.shape[0] // BLK
    nblk = base.shape[1] // BLK
    grid = jnp.zeros((tiles, nblk, BLK, BLK), jnp.float32)
    tile_ids = jnp.broadcast_to(jnp.arange(tiles, dtype=jnp.int32)[:, None], ids.shape)
    grid = grid.at[tile_ids, ids].add(sparse * live[:, :, None, None])
    full = grid.transpose(0, 2, 1, 3).reshape(base.shape)
    return (base.astype(jnp.float32) + full).astype(jnp.bfloat16)

def reference(tokens, cotangent, gate_weight, up_weight, down_weight, kept_blocks, kept_counts, sparse_delta, first_moment, second_moment):
    live = (jnp.arange(KMAX, dtype=jnp.int32)[None, None, :] < kept_counts[:, :, None]).astype(jnp.float32)
    gate_eff = patch_columns(gate_weight, sparse_delta[0], kept_blocks[0], live[0])
    up_eff = patch_columns(up_weight, sparse_delta[1], kept_blocks[1], live[1])
    down_eff = patch_rows(down_weight, sparse_delta[2], kept_blocks[2], live[2])
    gate = jnp.dot(tokens, gate_eff, preferred_element_type=jnp.float32)
    up = jnp.dot(tokens, up_eff, preferred_element_type=jnp.float32)
    sigma = jax.nn.sigmoid(gate)
    hidden = (gate * sigma * up).astype(jnp.bfloat16)
    hidden_grad = jnp.dot(cotangent, down_eff.T, preferred_element_type=jnp.float32)
    gate_grad = (hidden_grad * up * sigma * (1.0 + gate * (1.0 - sigma))).astype(jnp.bfloat16)
    up_grad = (hidden_grad * gate * sigma).astype(jnp.bfloat16)
    summed = jnp.dot(gate_grad, gate_eff.T, preferred_element_type=jnp.float32) + jnp.dot(up_grad, up_eff.T, preferred_element_type=jnp.float32)
    input_grad = summed.astype(jnp.bfloat16)
    rows = tokens.shape[0]
    nblk = D // BLK
    tiles = FF // BLK
    token_blocks = tokens.astype(jnp.float32).reshape(rows, nblk, BLK)
    cot_blocks = cotangent.astype(jnp.float32).reshape(rows, nblk, BLK)
    grad_gate = jnp.einsum('stka,stb->tkab', token_blocks[:, kept_blocks[0]], gate_grad.astype(jnp.float32).reshape(rows, tiles, BLK), precision=lax.Precision.HIGHEST)
    grad_up = jnp.einsum('stka,stb->tkab', token_blocks[:, kept_blocks[1]], up_grad.astype(jnp.float32).reshape(rows, tiles, BLK), precision=lax.Precision.HIGHEST)
    grad_down = jnp.einsum('sta,stkb->tkab', hidden.astype(jnp.float32).reshape(rows, tiles, BLK), cot_blocks[:, kept_blocks[2]], precision=lax.Precision.HIGHEST)
    grads = jnp.stack([grad_gate, grad_up, grad_down])
    mask = live[:, :, :, None, None]
    new_first = mask * (0.9 * first_moment + 0.1 * grads)
    new_second = mask * (0.999 * second_moment + 0.001 * grads * grads)
    new_delta = mask * (sparse_delta - 0.01 * new_first / (jnp.sqrt(new_second) + 1e-08))
    return (input_grad, new_delta, new_first, new_second)
```

```python
import functools

import jax
import jax.numpy as jnp
from jax import lax
from jax.experimental import pallas as pl
from jax.experimental.pallas import tpu as pltpu
from jax.sharding import PartitionSpec as P

BF16 = jnp.bfloat16
F32 = jnp.float32
MIB = 1 << 20
VMEM_SPEC = pl.BlockSpec(memory_space=pltpu.VMEM)
SMEM_SPEC = pl.BlockSpec(memory_space=pltpu.SMEM)
HBM_SPEC = pl.BlockSpec(memory_space=pltpu.HBM)


def dot_rows(left, right):
    return lax.dot_general(left, right, (((1,), (1,)), ((), ())), preferred_element_type=F32)


def dot_cols(left, right):
    return lax.dot_general(left, right, (((0,), (0,)), ((), ())), preferred_element_type=F32)


def chunk(i, size):
    return pl.ds(pl.multiple_of(i * size, size), size)


def params(limit):
    return pltpu.CompilerParams(vmem_limit_bytes=limit)


def add_block(ref, rows, cols, block):
    ref[rows, cols] = (ref[rows, cols].astype(F32) + block).astype(BF16)


def add_column_blocks(which, kept, counts, held, ref, first, size):
    tiles, slots, side = held.shape[1:4]
    for t in range(tiles):
        for k in range(slots):
            row = kept[which, t, k] * side

            @pl.when((k < counts[which, t]) & (row >= first) & (row < first + size))
            def _():
                rows = pl.ds(pl.multiple_of(row, side), side)
                add_block(ref, rows, slice(t * side, (t + 1) * side), held[which, t, k])


def side_by_side(array, kept, which, t, side, slots):
    return jnp.concatenate([array[:, chunk(kept[which, t, k], side)] for k in range(slots)], axis=1)


def layer_kernel(
    wide, step, kept, counts, tokens, cotangent, gate_weight, up_weight, down_weight, delta, first, second,
    keep, send, new_delta, new_first, new_second,
    gate_eff, up_eff, held, moments, ring, gate, up, hidden, gate_grad, up_grad,
    held_sems, in_sems, out_sems, ring_sems, part_sems,
):
    width, units = gate_eff.shape
    tiles, slots, side = held.shape[1:4]
    ahead = moments.shape[0] - 1
    half = keep.shape[0]
    depth, height, span = ring.shape
    across = width // span
    chunks = (units // height) * across

    def down_copy(c):
        source = down_weight.at[chunk(c // across, height), chunk(c % across, span)]
        return pltpu.make_async_copy(source, ring.at[c % depth], ring_sems.at[c % depth])

    def read_delta(which):
        return pltpu.make_async_copy(delta.at[which], held.at[which], held_sems.at[which])

    def read(a, t):
        slot = t % (ahead + 1)
        return pltpu.make_async_copy((first, second)[a].at[:, t], moments.at[slot, a], in_sems.at[slot, a])

    def write_delta(t):
        return pltpu.make_async_copy(held.at[:, t], new_delta.at[:, t], out_sems.at[2, t])

    def write(a, t):
        out = (new_first, new_second)[a]
        return pltpu.make_async_copy(moments.at[t % (ahead + 1), a], out.at[:, t], out_sems.at[a, t])

    parts = width // wide

    def part_copy(which, p):
        weight, out = ((gate_weight, gate_eff), (up_weight, up_eff))[which]
        rows = chunk(p, wide)
        return pltpu.make_async_copy(weight.at[rows], out.at[rows], part_sems.at[which, p])

    def forward(which, out, p, carry):
        part_copy(which, p).wait()
        eff = (gate_eff, up_eff)[which]

        @pl.when(p == 0)
        def _():
            read_delta(which).wait()
            out[...] = jnp.zeros_like(out)

        add_column_blocks(which, kept, counts, held, eff, p * wide, wide)
        part = chunk(p, wide)
        out[...] += jnp.dot(tokens[:, part], eff[part, :], preferred_element_type=F32)
        return carry

    read_delta(0).start()
    for p in range(parts):
        part_copy(0, p).start()
    read_delta(1).start()
    for p in range(parts):
        part_copy(1, p).start()
    read_delta(2).start()
    for c in range(min(depth, chunks)):
        down_copy(c).start()
    lax.fori_loop(0, parts, functools.partial(forward, 0, gate), 0)
    for t in range(min(ahead, tiles)):
        for a in range(2):
            read(a, t).start()
    lax.fori_loop(0, parts, functools.partial(forward, 1, up), 0)
    read_delta(2).wait()

    def backward(r, carry):
        hidden_grad = jnp.zeros((2 * half, height), F32)
        for q in range(across):
            c = r * across + q
            down_copy(c).wait()
            slot = ring.at[c % depth]
            for i in range(height // side):
                t = r * (height // side) + i
                for k in range(slots):
                    col = kept[2, t, k] * side - q * span

                    @pl.when((k < counts[2, t]) & (col >= 0) & (col < span))
                    def _():
                        cols = pl.ds(pl.multiple_of(col, side), side)
                        add_block(slot, slice(i * side, (i + 1) * side), cols, held[2, t, k])

            hidden_grad += dot_rows(cotangent[:, q * span : (q + 1) * span], slot[...])

            @pl.when(c + depth < chunks)
            def _():
                down_copy(c + depth).start()

        own = chunk(r, height)
        g, u = gate[:, own], up[:, own]
        sigma = jax.nn.sigmoid(g)
        silu = g * sigma
        hidden[:, own] = (silu * u).astype(BF16)
        gate_grad[:, own] = (hidden_grad * u * sigma * (1.0 + g * (1.0 - sigma))).astype(BF16)
        up_grad[:, own] = (hidden_grad * silu).astype(BF16)
        return carry

    lax.fori_loop(0, units // height, backward, 0)

    def input_part(i):
        part = chunk(i, step)
        both = dot_rows(gate_grad[...], gate_eff[part, :]) + dot_rows(up_grad[...], up_eff[part, :])
        keep[:, part] = both[:half]
        send[:, part] = both[half:].astype(BF16)

    def adam(t):
        own = chunk(t, side)
        slot = t % (ahead + 1)
        for a in range(2):
            read(a, t).wait()
        for which in range(3):
            if which == 2:
                grads = dot_cols(hidden[:, own], side_by_side(cotangent, kept, 2, t, side, slots))
            else:
                right = (gate_grad, up_grad)[which]
                grads = dot_cols(side_by_side(tokens, kept, which, t, side, slots), right[:, own])
            for k in range(slots):
                live = k < counts[which, t]
                part = slice(k * side, (k + 1) * side)
                grad = grads[:, part] if which == 2 else grads[part]
                m1 = 0.9 * moments[slot, 0, which, k] + 0.1 * grad
                m2 = 0.999 * moments[slot, 1, which, k] + 0.001 * grad * grad
                value = held[which, t, k] - 0.01 * m1 / (jnp.sqrt(m2) + 1e-08)
                held[which, t, k] = jnp.where(live, value, 0.0)
                moments[slot, 0, which, k] = jnp.where(live, m1, 0.0)
                moments[slot, 1, which, k] = jnp.where(live, m2, 0.0)
        write_delta(t).start()
        for a in range(2):
            write(a, t).start()

        @pl.when(t + ahead < tiles)
        def _():
            @pl.when(t >= 1)
            def _():
                for a in range(2):
                    write(a, t - 1).wait()

            for a in range(2):
                read(a, t + ahead).start()

    steps = width // step

    def last(i, carry):
        if steps == tiles:
            adam(i)
        input_part(i)
        return carry

    lax.fori_loop(0, steps, last, 0)
    if steps != tiles:
        lax.fori_loop(0, tiles, lambda t, carry: (adam(t), carry)[1], 0)
    for t in range(tiles):
        write_delta(t).wait()
    for t in range(max(tiles - ahead - 1, 0), tiles):
        for a in range(2):
            write(a, t).wait()


def layer(kept, counts, tokens, cotangent, gate_weight, up_weight, down_weight, arrays):
    rows, width = tokens.shape
    units = gate_weight.shape[1]
    shape = arrays[0].shape
    tiles, side = shape[1], shape[-1]
    height, span = min(2, tiles) * side, width // 2
    moment = jax.ShapeDtypeStruct(shape, F32)
    return pl.pallas_call(
        functools.partial(layer_kernel, min(width, 2048), min(width, 1024)),
        out_shape=(
            jax.ShapeDtypeStruct((rows // 2, width), F32),
            jax.ShapeDtypeStruct((rows // 2, width), BF16),
            moment,
            moment,
            moment,
        ),
        in_specs=[SMEM_SPEC] * 2 + [VMEM_SPEC] * 2 + [HBM_SPEC] * 6,
        out_specs=(VMEM_SPEC,) * 2 + (HBM_SPEC,) * 3,
        scratch_shapes=[
            pltpu.VMEM((width, units), BF16),
            pltpu.VMEM((width, units), BF16),
            pltpu.VMEM(shape, F32),
            pltpu.VMEM((4, 2, 3, *shape[2:]), F32),
            pltpu.VMEM((3, height, span), BF16),
            pltpu.VMEM((rows, units), F32),
            pltpu.VMEM((rows, units), F32),
            pltpu.VMEM((rows, units), BF16),
            pltpu.VMEM((rows, units), BF16),
            pltpu.VMEM((rows, units), BF16),
            pltpu.SemaphoreType.DMA((3,)),
            pltpu.SemaphoreType.DMA((4, 2)),
            pltpu.SemaphoreType.DMA((3, tiles)),
            pltpu.SemaphoreType.DMA((3,)),
            pltpu.SemaphoreType.DMA((2, width // min(width, 2048))),
        ],
        compiler_params=params(57 * MIB),
        cost_estimate=pl.CostEstimate(
            flops=10 * rows * width * units, bytes_accessed=10 * width * units, transcendentals=0
        ),
        name="layer",
    )(kept, counts, tokens, cotangent, gate_weight, up_weight, down_weight, *arrays)


def exchange(value, distance, size):
    return lax.ppermute(value, "dp", [(i, i ^ distance) for i in range(size)])


def exchange_order(size):
    distances = [1 << bit for bit in range(size.bit_length() - 1)]
    return distances[1:2] + distances[:1:-1] + distances[:1]


def on_device(
    size,
    tokens,
    cotangent,
    gate_weight,
    up_weight,
    down_weight,
    kept_blocks,
    kept_counts,
    sparse_delta,
    first_moment,
    second_moment,
):
    order = exchange_order(size)
    for distance in order:
        tokens = jnp.concatenate([tokens, exchange(tokens, distance, size)], 0)
    for distance in order:
        cotangent = jnp.concatenate([cotangent, exchange(cotangent, distance, size)], 0)
    arrays = (sparse_delta, first_moment, second_moment)
    total, away, *news = layer(
        kept_blocks, kept_counts, tokens, cotangent, gate_weight, up_weight, down_weight, arrays
    )
    for distance in order[::-1]:
        half = total.shape[0] // 2
        if distance != order[-1]:
            total, away = total[:half], total[half:].astype(BF16)
        total = total + exchange(away, distance, size).astype(F32)
    return (total.astype(BF16), *news)


def solution(mesh):
    rows = P(("groups", "dp"), None)
    blocks = P("groups", "dp", None, None, None)
    return jax.shard_map(
        functools.partial(on_device, mesh.shape["dp"]),
        mesh=mesh,
        in_specs=(
            rows,
            rows,
            P(None, "dp"),
            P(None, "dp"),
            P("dp", None),
            P("groups", "dp", None),
            P("groups", "dp"),
            blocks,
            blocks,
            blocks,
        ),
        out_specs=(rows, blocks, blocks, blocks),
        check_vma=False,
    )
```

```python
import functools

import jax
import jax.numpy as jnp
from jax import lax
from jax.experimental import pallas as pl
from jax.experimental.pallas import tpu as pltpu
from jax.sharding import PartitionSpec as P

BF16 = jnp.bfloat16
F32 = jnp.float32
MIB = 1 << 20
VMEM_SPEC = pl.BlockSpec(memory_space=pltpu.VMEM)
SMEM_SPEC = pl.BlockSpec(memory_space=pltpu.SMEM)
HBM_SPEC = pl.BlockSpec(memory_space=pltpu.HBM)


def in_hbm(*arrays):
    return [pltpu.with_memory_space_constraint(array, pltpu.HBM) for array in arrays]


def in_vmem(*arrays):
    return [pltpu.with_memory_space_constraint(array, pltpu.VMEM) for array in arrays]


def dot_rows(left, right):
    return lax.dot_general(left, right, (((1,), (1,)), ((), ())), preferred_element_type=F32)


def dot_cols(left, right):
    return lax.dot_general(left, right, (((0,), (0,)), ((), ())), preferred_element_type=F32)


def chunk(i, size):
    return pl.ds(pl.multiple_of(i * size, size), size)


def params(limit):
    return pltpu.CompilerParams(vmem_limit_bytes=limit)


def cost(flops, moved):
    return pl.CostEstimate(flops=flops, bytes_accessed=moved, transcendentals=0)


def add_block(ref, rows, cols, block):
    ref[rows, cols] = (ref[rows, cols].astype(F32) + block).astype(BF16)


def enter_kernel(count, *refs):
    blocks, targets, sems = refs[count], refs[count + 1 : -1], refs[-1]
    sources = [*refs[:count], *(blocks.at[i] for i in range(blocks.shape[0]))]
    copies = [
        pltpu.make_async_copy(source, target, sems.at[i])
        for i, (source, target) in enumerate(zip(sources, targets))
    ]
    for copy in copies:
        copy.start()
    for copy in copies:
        copy.wait()


def into_vmem(*arrays):
    *whole, blocks = arrays
    shapes = [array.shape for array in whole] + [blocks.shape[1:]] * blocks.shape[0]
    kinds = [array.dtype for array in whole] + [blocks.dtype] * blocks.shape[0]
    return pl.pallas_call(
        functools.partial(enter_kernel, len(whole)),
        out_shape=tuple(pltpu.VMEM(*out) for out in zip(shapes, kinds)),
        in_specs=[HBM_SPEC] * len(arrays),
        scratch_shapes=[pltpu.SemaphoreType.DMA((len(shapes),))],
        compiler_params=params(2 * MIB),
        name="enter",
    )(*in_hbm(*arrays))


def add_column_blocks(which, kept, counts, delta, ref, offset, first, size):
    tiles, slots, side = delta.shape[:3]
    for t in range(tiles):
        for k in range(slots):
            row = kept[which, k, t] * side - offset

            @pl.when((k < counts[which, t]) & (row >= first) & (row < first + size))
            def _():
                rows = pl.ds(pl.multiple_of(row, side), side)
                add_block(ref, rows, slice(t * side, (t + 1) * side), delta[t, k])


def patch_kernel(which, offset, step, kept, counts, delta, weight, out, sems):
    parts = out.shape[0] // step

    def part_copy(p):
        source = weight.at[pl.ds(offset + p * step, step)]
        return pltpu.make_async_copy(source, out.at[pl.ds(p * step, step)], sems.at[p])

    for p in range(parts):
        part_copy(p).start()
    for p in range(parts):
        part_copy(p).wait()
        add_column_blocks(which, kept, counts, delta, out, offset, p * step, step)


def patched(which, offset, height, kept, counts, delta, weight):
    units = weight.shape[1]
    step = height // 2
    return pl.pallas_call(
        functools.partial(patch_kernel, which, offset, step),
        out_shape=pltpu.VMEM((height, units), BF16),
        in_specs=[SMEM_SPEC, SMEM_SPEC, VMEM_SPEC, HBM_SPEC],
        scratch_shapes=[pltpu.SemaphoreType.DMA((height // step,))],
        compiler_params=params(4 * MIB),
        cost_estimate=cost(0, 2 * height * units),
        name="patch",
    )(kept, counts, *in_vmem(delta), *in_hbm(weight))


def moment_copies(which, sources, targets, sems, row=0):
    return [
        pltpu.make_async_copy(source.at[which], target, sems.at[i, row])
        for i, (source, target) in enumerate(zip(sources, targets))
    ]


def moments_kernel(which, first, second, first_out, second_out, sems):
    copies = moment_copies(which, (first, second), (first_out, second_out), sems)
    for copy in copies:
        copy.start()
    for copy in copies:
        copy.wait()


def moments(which, first, second):
    out = pltpu.VMEM(first.shape[1:], F32)
    return pl.pallas_call(
        functools.partial(moments_kernel, which),
        out_shape=(out, out),
        in_specs=[HBM_SPEC] * 2,
        scratch_shapes=[pltpu.SemaphoreType.DMA((2, 1))],
        compiler_params=params(2 * MIB),
        cost_estimate=cost(0, 8 * first[0].size),
        name="moments",
    )(*in_hbm(first, second))


def layer_kernel(
    wide, step, kept, counts, tokens_0, tokens_1, cotangent_0, cotangent_1,
    gate_0, gate_1, up_delta, down_delta, up_weight, down_weight, first, second,
    keep, send, tokens, cotangent, hidden, gate_grad, up_grad, *refs,
):
    moments_out = refs[:-7]
    up_eff, ring, gate, up, ring_sems, part_sems, moment_sems = refs[-7:]
    width, units = up_eff.shape
    tiles, slots, side = up_delta.shape[:3]
    half = keep.shape[0]
    depth, height, span = ring.shape
    across = width // span
    chunks = (units // height) * across

    def down_copy(c):
        source = down_weight.at[chunk(c // across, height), chunk(c % across, span)]
        return pltpu.make_async_copy(source, ring.at[c % depth], ring_sems.at[c % depth])

    lower = width // 2
    parts = width // wide
    flight = 3

    def part_copy(p):
        rows = chunk(p, wide)
        return pltpu.make_async_copy(up_weight.at[rows], up_eff.at[rows], part_sems.at[p])

    def start(j):
        @pl.when(j < parts)
        def _():
            part_copy(j).start()

        @pl.when((j >= parts) & (j < parts + min(depth, chunks)))
        def _():
            down_copy(j - parts).start()

    for j in range(flight):
        start(j)
    for whole, part_0, part_1 in (
        (tokens, tokens_0, tokens_1),
        (cotangent, cotangent_0, cotangent_1),
    ):
        whole[:half] = part_0[...]
        whole[half:] = part_1[...]
    gate[...] = jnp.zeros_like(gate)
    up[...] = jnp.zeros_like(up)

    def product(out, eff, first_part, i):
        left = tokens[:, chunk(first_part + i, wide)]
        out[...] += jnp.dot(left, eff[chunk(i, wide), :], preferred_element_type=F32)

    def forward_gate(eff, first_part, i, carry):
        product(gate, eff, first_part, i)
        return carry

    def forward_up(p, carry):
        part_copy(p).wait()
        start(p + flight)
        add_column_blocks(1, kept, counts, up_delta, up_eff, 0, p * wide, wide)
        product(up, up_eff, 0, p)
        return carry

    lax.fori_loop(0, parts // 2, functools.partial(forward_gate, gate_0, 0), 0)
    lax.fori_loop(0, parts // 2, functools.partial(forward_gate, gate_1, parts // 2), 0)
    lax.fori_loop(0, parts, forward_up, 0)

    def backward(r, carry):
        hidden_grad = jnp.zeros((2 * half, height), F32)
        for q in range(across):
            c = r * across + q
            down_copy(c).wait()
            slot = ring.at[c % depth]
            for i in range(height // side):
                t = r * (height // side) + i
                for k in range(slots):
                    col = kept[2, k, t] * side - q * span

                    @pl.when((k < counts[2, t]) & (col >= 0) & (col < span))
                    def _():
                        cols = pl.ds(pl.multiple_of(col, side), side)
                        add_block(slot, slice(i * side, (i + 1) * side), cols, down_delta[t, k])

            hidden_grad += dot_rows(cotangent[:, q * span : (q + 1) * span], slot[...])

            @pl.when(c + depth < chunks)
            def _():
                down_copy(c + depth).start()

        own = chunk(r, height)
        g, u = gate[:, own], up[:, own]
        sigma = jax.nn.sigmoid(g)
        silu = g * sigma
        hidden[:, own] = (silu * u).astype(BF16)
        gate_grad[:, own] = (hidden_grad * u * sigma * (1.0 + g * (1.0 - sigma))).astype(BF16)
        up_grad[:, own] = (hidden_grad * silu).astype(BF16)
        return carry

    lax.fori_loop(0, units // height, backward, 0)
    copies = []
    for which in range(len(moments_out) // 2):
        targets = moments_out[2 * which : 2 * which + 2]
        copies += moment_copies(which, (first, second), targets, moment_sems, which)
    for copy in copies:
        copy.start()

    def input_part(gate_eff, offset, i, carry):
        cols = chunk(offset // step + i, step)
        both = dot_rows(gate_grad[...], gate_eff[chunk(i, step), :])
        both += dot_rows(up_grad[...], up_eff[cols, :])
        keep[:, cols] = both[:half]
        send[:, cols] = both[half:].astype(BF16)
        return carry

    lax.fori_loop(0, lower // step, functools.partial(input_part, gate_0, 0), 0)
    lax.fori_loop(0, lower // step, functools.partial(input_part, gate_1, lower), 0)
    for copy in copies:
        copy.wait()


def layer(ahead, kept, counts, tokens, cotangent, gate_eff, deltas, up_weight, down_weight, first, second):
    rows, width = 2 * tokens[0].shape[0], tokens[0].shape[1]
    units = gate_eff[0].shape[1]
    shape = first.shape
    tiles, side = shape[1], shape[-1]
    height, span = min(2, tiles) * side, width // 2
    wide, step = width // 4, width // 8
    grad = pltpu.VMEM((rows, units), BF16)
    return pl.pallas_call(
        functools.partial(layer_kernel, wide, step),
        out_shape=(
            pltpu.VMEM((rows // 2, width), F32),
            pltpu.VMEM((rows // 2, width), BF16),
            pltpu.VMEM((rows, width), BF16),
            pltpu.VMEM((rows, width), BF16),
            grad,
            grad,
            grad,
            *(pltpu.VMEM(shape[1:], F32),) * (2 * ahead),
        ),
        in_specs=[SMEM_SPEC] * 2 + [VMEM_SPEC] * 8 + [HBM_SPEC] * 4,
        scratch_shapes=[
            pltpu.VMEM((width, units), BF16),
            pltpu.VMEM((3, height, span), BF16),
            pltpu.VMEM((rows, units), F32),
            pltpu.VMEM((rows, units), F32),
            pltpu.SemaphoreType.DMA((3,)),
            pltpu.SemaphoreType.DMA((width // wide,)),
            pltpu.SemaphoreType.DMA((2, max(ahead, 1))),
        ],
        compiler_params=params(25 * MIB),
        cost_estimate=cost(10 * rows * width * units, 10 * width * units),
        name="layer",
    )(
        kept,
        counts,
        *in_vmem(*tokens, *cotangent, *gate_eff, *deltas[1:]),
        *in_hbm(up_weight, down_weight, first, second),
    )


def adam_kernel(which, kept, counts, left, right, delta, first, second, *refs):
    outs = refs[-5:-2]
    made, sems = refs[-2:]
    tiles, slots, side = delta.shape[:3]

    def write(a, t):
        return pltpu.make_async_copy(made.at[a, t], outs[a].at[which, t], sems.at[a, t])

    def tile(t, carry):
        own = chunk(t, side)
        for k in range(slots):
            block = chunk(kept[which, k, t], side)
            if which == 2:
                grad = dot_cols(left[:, own], right[:, block])
            else:
                grad = dot_cols(left[:, block], right[:, own])
            live = k < counts[which, t]
            m1 = 0.9 * first[t, k] + 0.1 * grad
            m2 = 0.999 * second[t, k] + 0.001 * grad * grad
            value = delta[t, k] - 0.01 * m1 / (jnp.sqrt(m2) + 1e-08)
            for a, new in enumerate((value, m1, m2)):
                made[a, t, k] = jnp.where(live, new, 0.0)
        for a in range(3):
            write(a, t).start()
        return carry

    lax.fori_loop(0, tiles, tile, 0, unroll=min(tiles, 2))
    for t in range(tiles):
        for a in range(3):
            write(a, t).wait()


def adam(which, kept, counts, left, right, delta, moment_pair, done):
    shape = (3, *delta.shape)
    out = pltpu.HBM(shape, F32)
    return pl.pallas_call(
        functools.partial(adam_kernel, which),
        out_shape=(out, out, out),
        in_specs=[SMEM_SPEC] * 2 + [VMEM_SPEC] * 5 + [HBM_SPEC] * len(done),
        out_specs=(HBM_SPEC,) * 3,
        scratch_shapes=[pltpu.VMEM((3, *shape[1:]), F32), pltpu.SemaphoreType.DMA((3, shape[1]))],
        input_output_aliases={7 + i: i for i in range(len(done))},
        compiler_params=params(8 * MIB),
        cost_estimate=cost(0, 12 * delta.size),
        name="adam",
    )(kept, counts, *in_vmem(left, right, delta, *moment_pair), *in_hbm(*done))


def exchange(value, distance, size):
    return lax.ppermute(value, "dp", [(i, i ^ distance) for i in range(size)])


def exchange_order(size):
    distances = [1 << bit for bit in range(size.bit_length() - 1)]
    return distances[1:2] + distances[:1:-1] + distances[:1]


def after(value, *others):
    return lax.optimization_barrier((value, others))[0]


def on_device(
    size,
    tokens,
    cotangent,
    gate_weight,
    up_weight,
    down_weight,
    kept_blocks,
    kept_counts,
    sparse_delta,
    first_moment,
    second_moment,
):
    order = exchange_order(size)
    raw = (tokens, cotangent)
    tokens, cotangent, kept, counts, *deltas = into_vmem(
        tokens, cotangent, kept_blocks.transpose(0, 2, 1), kept_counts, sparse_delta
    )
    half = gate_weight.shape[0] // 2
    pair = (tokens, cotangent)
    gate_eff = []
    for i, distance in enumerate(order):
        got = tuple(exchange(rows, distance, size) for rows in (pair if i else raw))
        if max(len(order) - 3, 0) <= i < len(order) - 1:
            offset = len(gate_eff) * half
            gate_eff.append(patched(0, offset, half, after(kept, *pair), counts, deltas[0], gate_weight))
        if i < len(order) - 1:
            pair = tuple(jnp.concatenate(both, 0) for both in zip(pair, got))
            pair = after(pair, *deltas, *gate_eff[-1:])
    tokens, cotangent = zip(pair, got)
    ahead = 3
    total, away, tokens, cotangent, hidden, gate_grad, up_grad, *fetched = layer(
        ahead, kept, counts, tokens, cotangent, gate_eff, deltas, up_weight, down_weight, first_moment, second_moment
    )
    operands = ((tokens, gate_grad), (tokens, up_grad), (hidden, cotangent))
    news = ()
    for i, distance in enumerate(order[::-1]):
        if i:
            half = total.shape[0] // 2
            total, away = total[:half], total[half:].astype(BF16)
        got = exchange(away, distance, size)
        which = i - (len(order) - 3)
        if which == -1 or (which == 0 and i == 0):
            for late in range(ahead, 3):
                fetched += moments(late, after(first_moment, away), second_moment)
            got = after(got, *fetched)
        if which >= 0:
            pair = fetched[2 * which : 2 * which + 2]
            news = adam(which, after(kept, away), counts, *operands[which], deltas[which], pair, news)
        total = total + got.astype(F32)
        if which >= 0:
            total = after(total, *news)
    return (total.astype(BF16), *news)


def solution(mesh):
    rows = P(("groups", "dp"), None)
    blocks = P("groups", "dp", None, None, None)
    return jax.shard_map(
        functools.partial(on_device, mesh.shape["dp"]),
        mesh=mesh,
        in_specs=(
            rows,
            rows,
            P(None, "dp"),
            P(None, "dp"),
            P("dp", None),
            P("groups", "dp", None),
            P("groups", "dp"),
            blocks,
            blocks,
            blocks,
        ),
        out_specs=(rows, blocks, blocks, blocks),
        check_vma=False,
    )
```

```python
import functools

import jax
import jax.numpy as jnp
from jax import lax
from jax.experimental import pallas as pl
from jax.experimental.pallas import tpu as pltpu
from jax.sharding import PartitionSpec as P

BF16 = jnp.bfloat16
F32 = jnp.float32
MIB = 1 << 20
VMEM_SPEC = pl.BlockSpec(memory_space=pltpu.VMEM)
SMEM_SPEC = pl.BlockSpec(memory_space=pltpu.SMEM)
HBM_SPEC = pl.BlockSpec(memory_space=pltpu.HBM)


def in_hbm(*arrays):
    return [pltpu.with_memory_space_constraint(array, pltpu.HBM) for array in arrays]


def in_vmem(*arrays):
    return [pltpu.with_memory_space_constraint(array, pltpu.VMEM) for array in arrays]


def in_smem(*arrays):
    return [pltpu.with_memory_space_constraint(array, pltpu.SMEM) for array in arrays]


def dot_rows(left, right):
    return lax.dot_general(left, right, (((1,), (1,)), ((), ())), preferred_element_type=F32)


def dot_cols(left, right):
    return lax.dot_general(left, right, (((0,), (0,)), ((), ())), preferred_element_type=F32)


def chunk(i, size):
    return pl.ds(pl.multiple_of(i * size, size), size)


def params(limit):
    return pltpu.CompilerParams(vmem_limit_bytes=limit)


def cost(flops, moved):
    return pl.CostEstimate(flops=flops, bytes_accessed=moved, transcendentals=0)


def add_block(ref, rows, cols, block):
    ref[rows, cols] = (ref[rows, cols].astype(F32) + block).astype(BF16)


def enter_kernel(count, *refs):
    blocks, targets, sems = refs[count], refs[count + 1 : -1], refs[-1]
    sources = [*refs[:count], *(blocks.at[i] for i in range(blocks.shape[0]))]
    copies = [
        pltpu.make_async_copy(source, target, sems.at[i])
        for i, (source, target) in enumerate(zip(sources, targets))
    ]
    for copy in copies:
        copy.start()
    for copy in copies:
        copy.wait()


def into_vmem(*arrays):
    *whole, blocks = arrays
    shapes = [array.shape for array in whole] + [blocks.shape[1:]] * blocks.shape[0]
    kinds = [array.dtype for array in whole] + [blocks.dtype] * blocks.shape[0]
    return pl.pallas_call(
        functools.partial(enter_kernel, len(whole)),
        out_shape=tuple(
            (pltpu.SMEM if kind == jnp.int32 else pltpu.VMEM)(shape, kind)
            for shape, kind in zip(shapes, kinds)
        ),
        out_specs=tuple(SMEM_SPEC if kind == jnp.int32 else VMEM_SPEC for kind in kinds),
        in_specs=[HBM_SPEC] * len(arrays),
        scratch_shapes=[pltpu.SemaphoreType.DMA((len(shapes),))],
        compiler_params=params(2 * MIB),
        name="enter",
    )(*in_hbm(*arrays))


def add_column_blocks(which, kept, counts, delta, ref, offset, first, size):
    tiles, slots, side = delta.shape[:3]

    def tile(t, carry):
        for k in range(slots):
            row = kept[which, k, t] * side - offset

            @pl.when((k < counts[which, t]) & (row >= first) & (row < first + size))
            def _():
                rows = pl.ds(pl.multiple_of(row, side), side)
                add_block(ref, rows, chunk(t, side), delta[t, k])

        return carry

    lax.fori_loop(0, tiles, tile, 0)


def patch_kernel(which, offset, step, kept, counts, delta, weight, out, sems):
    parts = out.shape[0] // step

    def part_copy(p):
        source = weight.at[pl.ds(offset + p * step, step)]
        return pltpu.make_async_copy(source, out.at[pl.ds(p * step, step)], sems.at[p])

    for p in range(parts):
        part_copy(p).start()
    for p in range(parts):
        part_copy(p).wait()
        add_column_blocks(which, kept, counts, delta, out, offset, p * step, step)


def patched(which, offset, height, kept, counts, delta, weight):
    units = weight.shape[1]
    step = height // 4
    return pl.pallas_call(
        functools.partial(patch_kernel, which, offset, step),
        out_shape=pltpu.VMEM((height, units), BF16),
        in_specs=[SMEM_SPEC, SMEM_SPEC, VMEM_SPEC, HBM_SPEC],
        scratch_shapes=[pltpu.SemaphoreType.DMA((height // step,))],
        compiler_params=params(4 * MIB),
        cost_estimate=cost(0, 2 * height * units),
        name="patch",
    )(*in_smem(kept, counts), *in_vmem(delta), *in_hbm(weight))


def moment_copies(which, sources, targets, sems, row=0):
    return [
        pltpu.make_async_copy(source.at[which], target, sems.at[i, row])
        for i, (source, target) in enumerate(zip(sources, targets))
    ]


def moments_kernel(which, first, second, first_out, second_out, sems):
    copies = moment_copies(which, (first, second), (first_out, second_out), sems)
    for copy in copies:
        copy.start()
    for copy in copies:
        copy.wait()


def moments(which, first, second):
    out = pltpu.VMEM(first.shape[1:], F32)
    return pl.pallas_call(
        functools.partial(moments_kernel, which),
        out_shape=(out, out),
        in_specs=[HBM_SPEC] * 2,
        scratch_shapes=[pltpu.SemaphoreType.DMA((2, 1))],
        compiler_params=params(2 * MIB),
        cost_estimate=cost(0, 8 * first[0].size),
        name="moments",
    )(*in_hbm(first, second))


def layer_kernel(
    wide, step, kept, counts, tokens_0, tokens_1, cotangent_0, cotangent_1,
    gate_0, gate_1, up_delta, down_delta, up_weight, down_weight, first, second,
    keep, send, tokens, cotangent, hidden, gate_grad, up_grad, *refs,
):
    moments_out = refs[:-7]
    up_eff, ring, gate, up, ring_sems, part_sems, moment_sems = refs[-7:]
    width, units = up_eff.shape
    tiles, slots, side = up_delta.shape[:3]
    half = keep.shape[0]
    depth, height, span = ring.shape
    across = width // span
    chunks = (units // height) * across

    def down_copy(c):
        source = down_weight.at[chunk(c // across, height), chunk(c % across, span)]
        return pltpu.make_async_copy(source, ring.at[c % depth], ring_sems.at[c % depth])

    lower = width // 2
    parts = width // wide
    flight = 3

    def part_copy(p):
        rows = chunk(p, wide)
        return pltpu.make_async_copy(up_weight.at[rows], up_eff.at[rows], part_sems.at[p])

    def start(j):
        @pl.when(j < parts)
        def _():
            part_copy(j).start()

        @pl.when((j >= parts) & (j < parts + min(depth, chunks)))
        def _():
            down_copy(j - parts).start()

    for j in range(flight):
        start(j)
    for whole, part_0, part_1 in (
        (tokens, tokens_0, tokens_1),
        (cotangent, cotangent_0, cotangent_1),
    ):
        whole[:half] = part_0[...]
        whole[half:] = part_1[...]
    gate[...] = jnp.zeros_like(gate)
    up[...] = jnp.zeros_like(up)

    def product(out, eff, first_part, i):
        left = tokens[:, chunk(first_part + i, wide)]
        out[...] += jnp.dot(left, eff[chunk(i, wide), :], preferred_element_type=F32)

    def forward_gate(eff, first_part, i, carry):
        product(gate, eff, first_part, i)
        return carry

    def forward_up(p, carry):
        part_copy(p).wait()
        start(p + flight)
        add_column_blocks(1, kept, counts, up_delta, up_eff, 0, p * wide, wide)
        product(up, up_eff, 0, p)
        return carry

    lax.fori_loop(0, parts // 2, functools.partial(forward_gate, gate_0, 0), 0)
    lax.fori_loop(0, parts // 2, functools.partial(forward_gate, gate_1, parts // 2), 0)
    lax.fori_loop(0, parts, forward_up, 0)

    def backward(r, carry):
        hidden_grad = jnp.zeros((2 * half, height), F32)
        for q in range(across):
            c = r * across + q
            down_copy(c).wait()
            slot = ring.at[c % depth]
            for i in range(height // side):
                t = r * (height // side) + i
                for k in range(slots):
                    col = kept[2, k, t] * side - q * span

                    @pl.when((k < counts[2, t]) & (col >= 0) & (col < span))
                    def _():
                        cols = pl.ds(pl.multiple_of(col, side), side)
                        add_block(slot, slice(i * side, (i + 1) * side), cols, down_delta[t, k])

            hidden_grad += dot_rows(cotangent[:, q * span : (q + 1) * span], slot[...])

            @pl.when(c + depth < chunks)
            def _():
                down_copy(c + depth).start()

        own = chunk(r, height)
        g, u = gate[:, own], up[:, own]
        sigma = jax.nn.sigmoid(g)
        silu = g * sigma
        hidden[:, own] = (silu * u).astype(BF16)
        gate_grad[:, own] = (hidden_grad * u * sigma * (1.0 + g * (1.0 - sigma))).astype(BF16)
        up_grad[:, own] = (hidden_grad * silu).astype(BF16)
        return carry

    lax.fori_loop(0, units // height, backward, 0)
    copies = []
    for which in range(len(moments_out) // 2):
        targets = moments_out[2 * which : 2 * which + 2]
        copies += moment_copies(which, (first, second), targets, moment_sems, which)
    for copy in copies:
        copy.start()

    def input_part(gate_eff, offset, i, carry):
        cols = chunk(offset // step + i, step)
        both = dot_rows(gate_eff[chunk(i, step), :], gate_grad[...])
        both = (both + dot_rows(up_eff[cols, :], up_grad[...])).T
        keep[:, cols] = both[:half]
        send[:, cols] = both[half:].astype(BF16)
        return carry

    lax.fori_loop(0, lower // step, functools.partial(input_part, gate_0, 0), 0)
    lax.fori_loop(0, lower // step, functools.partial(input_part, gate_1, lower), 0)
    for copy in copies:
        copy.wait()


def layer(ahead, kept, counts, tokens, cotangent, gate_eff, deltas, up_weight, down_weight, first, second):
    rows, width = 2 * tokens[0].shape[0], tokens[0].shape[1]
    units = gate_eff[0].shape[1]
    shape = first.shape
    tiles, side = shape[1], shape[-1]
    height, span = min(2, tiles) * side, width // 2
    wide, step = width // 4, width // 4
    grad = pltpu.VMEM((rows, units), BF16)
    return pl.pallas_call(
        functools.partial(layer_kernel, wide, step),
        out_shape=(
            pltpu.VMEM((rows // 2, width), F32),
            pltpu.VMEM((rows // 2, width), BF16),
            pltpu.VMEM((rows, width), BF16),
            pltpu.VMEM((rows, width), BF16),
            grad,
            grad,
            grad,
            *(pltpu.VMEM(shape[1:], F32),) * (2 * ahead),
        ),
        in_specs=[SMEM_SPEC] * 2 + [VMEM_SPEC] * 8 + [HBM_SPEC] * 4,
        scratch_shapes=[
            pltpu.VMEM((width, units), BF16),
            pltpu.VMEM((3, height, span), BF16),
            pltpu.VMEM((rows, units), F32),
            pltpu.VMEM((rows, units), F32),
            pltpu.SemaphoreType.DMA((3,)),
            pltpu.SemaphoreType.DMA((width // wide,)),
            pltpu.SemaphoreType.DMA((2, max(ahead, 1))),
        ],
        compiler_params=params(25 * MIB),
        cost_estimate=cost(10 * rows * width * units, 10 * width * units),
        name="layer",
    )(
        *in_smem(kept, counts),
        *in_vmem(*tokens, *cotangent, *gate_eff, *deltas[1:]),
        *in_hbm(up_weight, down_weight, first, second),
    )


def adam_kernel(which, kept, counts, left, right, delta, first, second, *refs):
    outs = refs[-5:-2]
    made, sems = refs[-2:]
    tiles, slots, side = delta.shape[:3]

    def write(a, t):
        return pltpu.make_async_copy(made.at[a, t], outs[a].at[which, t], sems.at[a, t])

    def tile(t, carry):
        own = chunk(t, side)
        for k in range(slots):
            block = chunk(kept[which, k, t], side)
            if which == 2:
                grad = dot_cols(left[:, own], right[:, block])
            else:
                grad = dot_cols(left[:, block], right[:, own])
            live = k < counts[which, t]
            m1 = 0.9 * first[t, k] + 0.1 * grad
            m2 = 0.999 * second[t, k] + 0.001 * grad * grad
            value = delta[t, k] - 0.01 * m1 / (jnp.sqrt(m2) + 1e-08)
            for a, new in enumerate((value, m1, m2)):
                made[a, t, k] = jnp.where(live, new, 0.0)
        for a in range(3):
            write(a, t).start()
        return carry

    lax.fori_loop(0, tiles, tile, 0, unroll=min(tiles, 2))
    for t in range(tiles):
        for a in range(3):
            write(a, t).wait()


def adam(which, kept, counts, left, right, delta, moment_pair, done):
    shape = (3, *delta.shape)
    out = pltpu.HBM(shape, F32)
    return pl.pallas_call(
        functools.partial(adam_kernel, which),
        out_shape=(out, out, out),
        in_specs=[SMEM_SPEC] * 2 + [VMEM_SPEC] * 5 + [HBM_SPEC] * len(done),
        out_specs=(HBM_SPEC,) * 3,
        scratch_shapes=[pltpu.VMEM((3, *shape[1:]), F32), pltpu.SemaphoreType.DMA((3, shape[1]))],
        input_output_aliases={7 + i: i for i in range(len(done))},
        compiler_params=params(8 * MIB),
        cost_estimate=cost(0, 12 * delta.size),
        name="adam",
    )(*in_smem(kept, counts), *in_vmem(left, right, delta, *moment_pair), *in_hbm(*done))


def exchange(value, distance, size):
    return lax.ppermute(value, "dp", [(i, i ^ distance) for i in range(size)])


def exchange_order(size):
    distances = [1 << bit for bit in range(size.bit_length() - 1)]
    return distances[::-1]


def after(value, *others):
    return lax.optimization_barrier((value, others))[0]


def on_device(
    size,
    tokens,
    cotangent,
    gate_weight,
    up_weight,
    down_weight,
    kept_blocks,
    kept_counts,
    sparse_delta,
    first_moment,
    second_moment,
):
    order = exchange_order(size)
    raw = (tokens, cotangent)
    tokens, cotangent, kept, counts, *deltas = into_vmem(
        tokens, cotangent, kept_blocks.transpose(0, 2, 1), kept_counts, sparse_delta
    )
    half = gate_weight.shape[0] // 2
    pair = (tokens, cotangent)
    gate_eff = []
    for i, distance in enumerate(order):
        got = tuple(exchange(rows, distance, size) for rows in (pair if i else raw))
        if max(len(order) - 3, 0) <= i < len(order) - 1:
            offset = len(gate_eff) * half
            gate_eff.append(patched(0, offset, half, after(kept, *pair), counts, deltas[0], gate_weight))
        if i < len(order) - 1:
            pair = tuple(jnp.concatenate(both, 0) for both in zip(pair, got))
            pair = after(pair, *deltas, *gate_eff[-1:])
    tokens, cotangent = zip(pair, got)
    ahead = 3
    total, away, tokens, cotangent, hidden, gate_grad, up_grad, *fetched = layer(
        ahead, kept, counts, tokens, cotangent, gate_eff, deltas, up_weight, down_weight, first_moment, second_moment
    )
    operands = ((tokens, gate_grad), (tokens, up_grad), (hidden, cotangent))
    news = ()
    for i, distance in enumerate(order[::-1]):
        if i:
            half = total.shape[0] // 2
            total, away = total[:half], total[half:].astype(BF16)
        got = exchange(away, distance, size)
        which = i - (len(order) - 3)
        if which == -1 or (which == 0 and i == 0):
            for late in range(ahead, 3):
                fetched += moments(late, after(first_moment, away), second_moment)
            got = after(got, *fetched)
        if which >= 0:
            pair = fetched[2 * which : 2 * which + 2]
            news = adam(which, after(kept, away), counts, *operands[which], deltas[which], pair, news)
        total = total + got.astype(F32)
        if which >= 0:
            total = after(total, *news)
    return (total.astype(BF16), *news)


def solution(mesh):
    rows = P(("groups", "dp"), None)
    blocks = P("groups", "dp", None, None, None)
    return jax.shard_map(
        functools.partial(on_device, mesh.shape["dp"]),
        mesh=mesh,
        in_specs=(
            rows,
            rows,
            P(None, "dp"),
            P(None, "dp"),
            P("dp", None),
            P("groups", "dp", None),
            P("groups", "dp"),
            blocks,
            blocks,
            blocks,
        ),
        out_specs=(rows, blocks, blocks, blocks),
        check_vma=False,
    )
```

```python
import functools

import jax
import jax.numpy as jnp
from jax import lax
from jax.experimental import pallas as pl
from jax.experimental.pallas import tpu as pltpu
from jax.sharding import PartitionSpec as P

BF16 = jnp.bfloat16
F32 = jnp.float32
MIB = 1 << 20
VMEM_SPEC = pl.BlockSpec(memory_space=pltpu.VMEM)
SMEM_SPEC = pl.BlockSpec(memory_space=pltpu.SMEM)
HBM_SPEC = pl.BlockSpec(memory_space=pltpu.HBM)


def in_hbm(*arrays):
    return [pltpu.with_memory_space_constraint(array, pltpu.HBM) for array in arrays]


def in_vmem(*arrays):
    return [pltpu.with_memory_space_constraint(array, pltpu.VMEM) for array in arrays]


def in_smem(*arrays):
    return [pltpu.with_memory_space_constraint(array, pltpu.SMEM) for array in arrays]


def dot_rows(left, right):
    return lax.dot_general(left, right, (((1,), (1,)), ((), ())), preferred_element_type=F32)


def dot_cols(left, right):
    return lax.dot_general(left, right, (((0,), (0,)), ((), ())), preferred_element_type=F32)


def chunk(i, size):
    return pl.ds(pl.multiple_of(i * size, size), size)


def params(limit):
    return pltpu.CompilerParams(vmem_limit_bytes=limit)


def cost(flops, moved):
    return pl.CostEstimate(flops=flops, bytes_accessed=moved, transcendentals=0)


def add_block(ref, rows, cols, block):
    ref[rows, cols] = (ref[rows, cols].astype(F32) + block).astype(BF16)


PARTS = 8


def list_live(per_part, kept, counts, begins, entries):
    _, slots, tiles = kept.shape
    for m in range(entries.shape[0]):

        def each(step, m=m):
            def tile(t, carry):
                for k in range(slots):

                    @pl.when(k < counts[m, t])
                    def _():
                        step(lax.div(kept[m, k, t], per_part), t * slots + k)

                return carry

            lax.fori_loop(0, tiles, tile, 0)

        def count(part, entry, m=m):
            begins[m, part + 1] += 1

        def place(part, entry, m=m):
            at = begins[m, part]
            entries[m, at] = entry
            begins[m, part] = at + 1

        for part in range(PARTS + 1):
            begins[m, part] = 0
        each(count)
        for part in range(PARTS):
            begins[m, part + 1] += begins[m, part]
        each(place)
        for part in range(PARTS, 0, -1):
            begins[m, part] = begins[m, part - 1]
        begins[m, 0] = 0


def enter_kernel(per_part, count, *refs):
    blocks, targets, sems = refs[count], refs[count + 1 : -3], refs[-1]
    begins, entries = refs[-3:-1]
    sources = [*refs[:count], *(blocks.at[i] for i in range(blocks.shape[0]))]
    copies = [
        pltpu.make_async_copy(source, target, sems.at[i])
        for i, (source, target) in enumerate(zip(sources, targets))
    ]
    for copy in copies:
        copy.start()
    for copy in copies[:count]:
        copy.wait()
    list_live(per_part, targets[count - 2], targets[count - 1], begins, entries)
    for copy in copies[count:]:
        copy.wait()


def into_vmem(*arrays):
    *whole, blocks = arrays
    _, tiles, slots, side, _ = blocks.shape
    shapes = [array.shape for array in whole] + [blocks.shape[1:]] * blocks.shape[0]
    kinds = [array.dtype for array in whole] + [blocks.dtype] * blocks.shape[0]
    shapes += [(2, PARTS + 1), (2, tiles * slots)]
    kinds += [jnp.int32] * 2
    per_part = whole[0].shape[1] // (PARTS * side)
    return pl.pallas_call(
        functools.partial(enter_kernel, per_part, len(whole)),
        out_shape=tuple(
            (pltpu.SMEM if kind == jnp.int32 else pltpu.VMEM)(shape, kind)
            for shape, kind in zip(shapes, kinds)
        ),
        out_specs=tuple(SMEM_SPEC if kind == jnp.int32 else VMEM_SPEC for kind in kinds),
        in_specs=[HBM_SPEC] * len(arrays),
        scratch_shapes=[pltpu.SemaphoreType.DMA((len(shapes) - 2,))],
        compiler_params=params(2 * MIB),
        name="enter",
    )(*in_hbm(*arrays))


def add_column_blocks(which, kept, begins, entries, delta, ref, offset, part, span):
    slots, side = delta.shape[1:3]

    def add(i, carry):
        entry = entries[which, i]
        t, k = lax.div(entry, slots), lax.rem(entry, slots)
        row = kept[which, k, t] * side - offset
        add_block(ref, pl.ds(pl.multiple_of(row, side), side), chunk(t, side), delta[t, k])
        return carry

    lax.fori_loop(begins[which, part], begins[which, part + span], add, 0)


def patch_kernel(which, offset, step, kept, begins, entries, delta, weight, out, sems):
    parts = out.shape[0] // step

    def part_copy(p):
        source = weight.at[pl.ds(offset + p * step, step)]
        return pltpu.make_async_copy(source, out.at[pl.ds(p * step, step)], sems.at[p])

    for p in range(parts):
        part_copy(p).start()
    for p in range(parts):
        part_copy(p).wait()
        add_column_blocks(which, kept, begins, entries, delta, out, offset, offset // step + p, 1)


def patched(which, offset, height, kept, lists, delta, weight):
    units = weight.shape[1]
    step = weight.shape[0] // PARTS
    return pl.pallas_call(
        functools.partial(patch_kernel, which, offset, step),
        out_shape=pltpu.VMEM((height, units), BF16),
        in_specs=[SMEM_SPEC] * 3 + [VMEM_SPEC, HBM_SPEC],
        scratch_shapes=[pltpu.SemaphoreType.DMA((height // step,))],
        compiler_params=params(4 * MIB),
        cost_estimate=cost(0, 2 * height * units),
        name="patch",
    )(*in_smem(kept, *lists), *in_vmem(delta), *in_hbm(weight))


def moment_copies(which, sources, targets, sems, row=0):
    return [
        pltpu.make_async_copy(source.at[which], target, sems.at[i, row])
        for i, (source, target) in enumerate(zip(sources, targets))
    ]


def moments_kernel(which, first, second, first_out, second_out, sems):
    copies = moment_copies(which, (first, second), (first_out, second_out), sems)
    for copy in copies:
        copy.start()
    for copy in copies:
        copy.wait()


def moments(which, first, second):
    out = pltpu.VMEM(first.shape[1:], F32)
    return pl.pallas_call(
        functools.partial(moments_kernel, which),
        out_shape=(out, out),
        in_specs=[HBM_SPEC] * 2,
        scratch_shapes=[pltpu.SemaphoreType.DMA((2, 1))],
        compiler_params=params(2 * MIB),
        cost_estimate=cost(0, 8 * first[0].size),
        name="moments",
    )(*in_hbm(first, second))


def layer_kernel(
    wide, step, kept, counts, begins, entries, tokens_0, tokens_1, cotangent_0, cotangent_1,
    gate_0, gate_1, up_delta, down_delta, up_weight, down_weight, first, second,
    keep, send, tokens, cotangent, hidden, gate_grad, up_grad, *refs,
):
    moments_out = refs[:-7]
    up_eff, ring, gate, up, ring_sems, part_sems, moment_sems = refs[-7:]
    width, units = up_eff.shape
    tiles, slots, side = up_delta.shape[:3]
    half = keep.shape[0]
    depth, height, span = ring.shape
    across = width // span
    chunks = (units // height) * across

    def down_copy(c):
        source = down_weight.at[chunk(c // across, height), chunk(c % across, span)]
        return pltpu.make_async_copy(source, ring.at[c % depth], ring_sems.at[c % depth])

    lower = width // 2
    parts = width // wide
    flight = 3

    def part_copy(p):
        rows = chunk(p, wide)
        return pltpu.make_async_copy(up_weight.at[rows], up_eff.at[rows], part_sems.at[p])

    def start(j):
        @pl.when(j < parts)
        def _():
            part_copy(j).start()

        @pl.when((j >= parts) & (j < parts + min(depth, chunks)))
        def _():
            down_copy(j - parts).start()

    for j in range(flight):
        start(j)
    for whole, part_0, part_1 in (
        (tokens, tokens_0, tokens_1),
        (cotangent, cotangent_0, cotangent_1),
    ):
        whole[:half] = part_0[...]
        whole[half:] = part_1[...]
    gate[...] = jnp.zeros_like(gate)
    up[...] = jnp.zeros_like(up)

    def product(out, eff, first_part, i):
        left = tokens[:, chunk(first_part + i, wide)]
        out[...] += jnp.dot(left, eff[chunk(i, wide), :], preferred_element_type=F32)

    def forward_gate(eff, first_part, i, carry):
        product(gate, eff, first_part, i)
        return carry

    def forward_up(p, carry):
        part_copy(p).wait()
        start(p + flight)
        span = wide * PARTS // width
        add_column_blocks(1, kept, begins, entries, up_delta, up_eff, 0, p * span, span)
        product(up, up_eff, 0, p)
        return carry

    lax.fori_loop(0, parts // 2, functools.partial(forward_gate, gate_0, 0), 0)
    lax.fori_loop(0, parts // 2, functools.partial(forward_gate, gate_1, parts // 2), 0)
    lax.fori_loop(0, parts, forward_up, 0)

    def backward(r, carry):
        hidden_grad = jnp.zeros((2 * half, height), F32)
        for q in range(across):
            c = r * across + q
            down_copy(c).wait()
            slot = ring.at[c % depth]
            for i in range(height // side):
                t = r * (height // side) + i
                for k in range(slots):
                    col = kept[2, k, t] * side - q * span

                    @pl.when((k < counts[2, t]) & (col >= 0) & (col < span))
                    def _():
                        cols = pl.ds(pl.multiple_of(col, side), side)
                        add_block(slot, slice(i * side, (i + 1) * side), cols, down_delta[t, k])

            hidden_grad += dot_rows(cotangent[:, q * span : (q + 1) * span], slot[...])

            @pl.when(c + depth < chunks)
            def _():
                down_copy(c + depth).start()

        own = chunk(r, height)
        g, u = gate[:, own], up[:, own]
        sigma = jax.nn.sigmoid(g)
        silu = g * sigma
        hidden[:, own] = (silu * u).astype(BF16)
        gate_grad[:, own] = (hidden_grad * u * sigma * (1.0 + g * (1.0 - sigma))).astype(BF16)
        up_grad[:, own] = (hidden_grad * silu).astype(BF16)
        return carry

    lax.fori_loop(0, units // height, backward, 0)
    copies = []
    for which in range(len(moments_out) // 2):
        targets = moments_out[2 * which : 2 * which + 2]
        copies += moment_copies(which, (first, second), targets, moment_sems, which)
    for copy in copies:
        copy.start()

    def input_part(gate_eff, offset, i, carry):
        cols = chunk(offset // step + i, step)
        both = dot_rows(gate_eff[chunk(i, step), :], gate_grad[...])
        both = (both + dot_rows(up_eff[cols, :], up_grad[...])).T
        keep[:, cols] = both[:half]
        send[:, cols] = both[half:].astype(BF16)
        return carry

    lax.fori_loop(0, lower // step, functools.partial(input_part, gate_0, 0), 0)
    lax.fori_loop(0, lower // step, functools.partial(input_part, gate_1, lower), 0)
    for copy in copies:
        copy.wait()


def layer(ahead, kept, counts, lists, tokens, cotangent, gate_eff, deltas, up_weight, down_weight, first, second):
    rows, width = 2 * tokens[0].shape[0], tokens[0].shape[1]
    units = gate_eff[0].shape[1]
    shape = first.shape
    tiles, side = shape[1], shape[-1]
    height, span = min(2, tiles) * side, width // 2
    wide, step = width // 4, width // 4
    grad = pltpu.VMEM((rows, units), BF16)
    return pl.pallas_call(
        functools.partial(layer_kernel, wide, step),
        out_shape=(
            pltpu.VMEM((rows // 2, width), F32),
            pltpu.VMEM((rows // 2, width), BF16),
            pltpu.VMEM((rows, width), BF16),
            pltpu.VMEM((rows, width), BF16),
            grad,
            grad,
            grad,
            *(pltpu.VMEM(shape[1:], F32),) * (2 * ahead),
        ),
        in_specs=[SMEM_SPEC] * 4 + [VMEM_SPEC] * 8 + [HBM_SPEC] * 4,
        scratch_shapes=[
            pltpu.VMEM((width, units), BF16),
            pltpu.VMEM((3, height, span), BF16),
            pltpu.VMEM((rows, units), F32),
            pltpu.VMEM((rows, units), F32),
            pltpu.SemaphoreType.DMA((3,)),
            pltpu.SemaphoreType.DMA((width // wide,)),
            pltpu.SemaphoreType.DMA((2, max(ahead, 1))),
        ],
        compiler_params=params(25 * MIB),
        cost_estimate=cost(10 * rows * width * units, 10 * width * units),
        name="layer",
    )(
        *in_smem(kept, counts, *lists),
        *in_vmem(*tokens, *cotangent, *gate_eff, *deltas[1:]),
        *in_hbm(up_weight, down_weight, first, second),
    )


def adam_kernel(which, kept, counts, left, right, delta, first, second, *refs):
    outs = refs[-5:-2]
    made, sems = refs[-2:]
    tiles, slots, side = delta.shape[:3]

    def write(a, t):
        return pltpu.make_async_copy(made.at[a, t], outs[a].at[which, t], sems.at[a, t])

    def tile(t, carry):
        own = chunk(t, side)
        for k in range(slots):
            block = chunk(kept[which, k, t], side)
            if which == 2:
                grad = dot_cols(left[:, own], right[:, block])
            else:
                grad = dot_cols(left[:, block], right[:, own])
            live = k < counts[which, t]
            m1 = 0.9 * first[t, k] + 0.1 * grad
            m2 = 0.999 * second[t, k] + 0.001 * grad * grad
            value = delta[t, k] - 0.01 * m1 / (jnp.sqrt(m2) + 1e-08)
            for a, new in enumerate((value, m1, m2)):
                made[a, t, k] = jnp.where(live, new, 0.0)
        for a in range(3):
            write(a, t).start()
        return carry

    lax.fori_loop(0, tiles, tile, 0, unroll=min(tiles, 2))
    for t in range(tiles):
        for a in range(3):
            write(a, t).wait()


def adam(which, kept, counts, left, right, delta, moment_pair, done):
    shape = (3, *delta.shape)
    out = pltpu.HBM(shape, F32)
    return pl.pallas_call(
        functools.partial(adam_kernel, which),
        out_shape=(out, out, out),
        in_specs=[SMEM_SPEC] * 2 + [VMEM_SPEC] * 5 + [HBM_SPEC] * len(done),
        out_specs=(HBM_SPEC,) * 3,
        scratch_shapes=[pltpu.VMEM((3, *shape[1:]), F32), pltpu.SemaphoreType.DMA((3, shape[1]))],
        input_output_aliases={7 + i: i for i in range(len(done))},
        compiler_params=params(8 * MIB),
        cost_estimate=cost(0, 12 * delta.size),
        name="adam",
    )(*in_smem(kept, counts), *in_vmem(left, right, delta, *moment_pair), *in_hbm(*done))


def exchange(value, distance, size):
    return lax.ppermute(value, "dp", [(i, i ^ distance) for i in range(size)])


def exchange_order(size):
    distances = [1 << bit for bit in range(size.bit_length() - 1)]
    return distances[::-1], distances[1:2] + distances[:1:-1] + distances[:1]


def joined(own, got, early):
    if not early:
        return jnp.concatenate([own, got], 0)
    half = own.shape[0] // 2
    return jnp.concatenate([own[:half], got[:half], own[half:], got[half:]], 0)


def after(value, *others):
    return lax.optimization_barrier((value, others))[0]


def on_device(
    size,
    tokens,
    cotangent,
    gate_weight,
    up_weight,
    down_weight,
    kept_blocks,
    kept_counts,
    sparse_delta,
    first_moment,
    second_moment,
):
    order, other_order = exchange_order(size)
    raw = (tokens, cotangent)
    tokens, cotangent, kept, counts, *deltas, begins, entries = into_vmem(
        tokens, cotangent, kept_blocks.transpose(0, 2, 1), kept_counts, sparse_delta
    )
    half = gate_weight.shape[0] // 2
    lists = (begins, entries)
    pair = (tokens, cotangent)
    gate_eff = []
    for i, distances in enumerate(zip(order, other_order)):
        sent = pair if i else raw
        got = tuple(exchange(rows, distance, size) for rows, distance in zip(sent, distances))
        if max(len(order) - 3, 0) <= i < len(order) - 1:
            offset = len(gate_eff) * half
            gate_eff.append(patched(0, offset, half, after(kept, *pair), lists, deltas[0], gate_weight))
        if i < len(order) - 1:
            pair = (joined(pair[0], got[0], False), joined(pair[1], got[1], i > 0))
            pair = after(pair, *deltas, *lists, *gate_eff[-1:])
    tokens, cotangent = zip(pair, got)
    ahead = 3
    total, away, tokens, cotangent, hidden, gate_grad, up_grad, *fetched = layer(
        ahead, kept, counts, lists, tokens, cotangent, gate_eff, deltas, up_weight, down_weight, first_moment, second_moment
    )
    operands = ((tokens, gate_grad), (tokens, up_grad), (hidden, cotangent))
    news = ()
    for i, distance in enumerate(order[::-1]):
        if i:
            half = total.shape[0] // 2
            total, away = total[:half], total[half:].astype(BF16)
        got = exchange(away, distance, size)
        which = i - (len(order) - 3)
        if which == -1 or (which == 0 and i == 0):
            for late in range(ahead, 3):
                fetched += moments(late, after(first_moment, away), second_moment)
            got = after(got, *fetched)
        if which >= 0:
            pair = fetched[2 * which : 2 * which + 2]
            news = adam(which, after(kept, away), counts, *operands[which], deltas[which], pair, news)
        total = total + got.astype(F32)
        if which >= 0:
            total = after(total, *news)
    return (total.astype(BF16), *news)


def solution(mesh):
    rows = P(("groups", "dp"), None)
    blocks = P("groups", "dp", None, None, None)
    return jax.shard_map(
        functools.partial(on_device, mesh.shape["dp"]),
        mesh=mesh,
        in_specs=(
            rows,
            rows,
            P(None, "dp"),
            P(None, "dp"),
            P("dp", None),
            P("groups", "dp", None),
            P("groups", "dp"),
            blocks,
            blocks,
            blocks,
        ),
        out_specs=(rows, blocks, blocks, blocks),
        check_vma=False,
    )
```

```python
import functools

import jax
import jax.numpy as jnp
from jax import lax
from jax.experimental import pallas as pl
from jax.experimental.pallas import tpu as pltpu
from jax.sharding import PartitionSpec as P

BF16 = jnp.bfloat16
F32 = jnp.float32
MIB = 1 << 20
VMEM_SPEC = pl.BlockSpec(memory_space=pltpu.VMEM)
SMEM_SPEC = pl.BlockSpec(memory_space=pltpu.SMEM)
HBM_SPEC = pl.BlockSpec(memory_space=pltpu.HBM)


def in_hbm(*arrays):
    return [pltpu.with_memory_space_constraint(array, pltpu.HBM) for array in arrays]


def in_vmem(*arrays):
    return [pltpu.with_memory_space_constraint(array, pltpu.VMEM) for array in arrays]


def in_smem(*arrays):
    return [pltpu.with_memory_space_constraint(array, pltpu.SMEM) for array in arrays]


def dot_rows(left, right):
    return lax.dot_general(left, right, (((1,), (1,)), ((), ())), preferred_element_type=F32)


def dot_cols(left, right):
    return lax.dot_general(left, right, (((0,), (0,)), ((), ())), preferred_element_type=F32)


def chunk(i, size):
    return pl.ds(pl.multiple_of(i * size, size), size)


def params(limit):
    return pltpu.CompilerParams(vmem_limit_bytes=limit)


def cost(flops, moved):
    return pl.CostEstimate(flops=flops, bytes_accessed=moved, transcendentals=0)


def add_block(ref, rows, cols, block):
    ref[rows, cols] = (ref[rows, cols].astype(F32) + block).astype(BF16)


PARTS = 8


def list_live(per_part, kept, counts, begins, entries):
    _, slots, tiles = kept.shape
    for m in range(entries.shape[0]):

        def each(step, m=m):
            def tile(t, carry):
                for k in range(slots):

                    @pl.when(k < counts[m, t])
                    def _():
                        step(lax.div(kept[m, k, t], per_part), t * slots + k)

                return carry

            lax.fori_loop(0, tiles, tile, 0)

        def count(part, entry, m=m):
            begins[m, part + 1] += 1

        def place(part, entry, m=m):
            at = begins[m, part]
            entries[m, at] = entry
            begins[m, part] = at + 1

        for part in range(PARTS + 1):
            begins[m, part] = 0
        each(count)
        for part in range(PARTS):
            begins[m, part + 1] += begins[m, part]
        each(place)
        for part in range(PARTS, 0, -1):
            begins[m, part] = begins[m, part - 1]
        begins[m, 0] = 0


def enter_kernel(per_part, count, *refs):
    blocks, targets, sems = refs[count], refs[count + 1 : -3], refs[-1]
    begins, entries = refs[-3:-1]
    sources = [*refs[:count], *(blocks.at[i] for i in range(blocks.shape[0]))]
    copies = [
        pltpu.make_async_copy(source, target, sems.at[i])
        for i, (source, target) in enumerate(zip(sources, targets))
    ]
    for copy in copies:
        copy.start()
    for copy in copies[:count]:
        copy.wait()
    list_live(per_part, targets[count - 2], targets[count - 1], begins, entries)
    for copy in copies[count:]:
        copy.wait()


def into_vmem(*arrays):
    *whole, blocks = arrays
    _, tiles, slots, side, _ = blocks.shape
    shapes = [array.shape for array in whole] + [blocks.shape[1:]] * blocks.shape[0]
    kinds = [array.dtype for array in whole] + [blocks.dtype] * blocks.shape[0]
    shapes += [(2, PARTS + 1), (2, tiles * slots)]
    kinds += [jnp.int32] * 2
    per_part = whole[0].shape[1] // (PARTS * side)
    return pl.pallas_call(
        functools.partial(enter_kernel, per_part, len(whole)),
        out_shape=tuple(
            (pltpu.SMEM if kind == jnp.int32 else pltpu.VMEM)(shape, kind)
            for shape, kind in zip(shapes, kinds)
        ),
        out_specs=tuple(SMEM_SPEC if kind == jnp.int32 else VMEM_SPEC for kind in kinds),
        in_specs=[HBM_SPEC] * len(arrays),
        scratch_shapes=[pltpu.SemaphoreType.DMA((len(shapes) - 2,))],
        compiler_params=params(2 * MIB),
        name="enter",
    )(*in_hbm(*arrays))


def add_column_blocks(which, kept, begins, entries, delta, ref, offset, part, span):
    slots, side = delta.shape[1:3]

    def add(i, carry):
        entry = entries[which, i]
        t, k = lax.div(entry, slots), lax.rem(entry, slots)
        row = kept[which, k, t] * side - offset
        add_block(ref, pl.ds(pl.multiple_of(row, side), side), chunk(t, side), delta[t, k])
        return carry

    lax.fori_loop(begins[which, part], begins[which, part + span], add, 0)


def patch_kernel(which, offset, step, kept, begins, entries, delta, weight, out, sems):
    parts = out.shape[0] // step

    def part_copy(p):
        source = weight.at[pl.ds(offset + p * step, step)]
        return pltpu.make_async_copy(source, out.at[pl.ds(p * step, step)], sems.at[p])

    for p in range(parts):
        part_copy(p).start()
    for p in range(parts):
        part_copy(p).wait()
        add_column_blocks(which, kept, begins, entries, delta, out, offset, offset // step + p, 1)


def patched(which, offset, height, kept, lists, delta, weight):
    units = weight.shape[1]
    step = weight.shape[0] // PARTS
    return pl.pallas_call(
        functools.partial(patch_kernel, which, offset, step),
        out_shape=pltpu.VMEM((height, units), BF16),
        in_specs=[SMEM_SPEC] * 3 + [VMEM_SPEC, HBM_SPEC],
        scratch_shapes=[pltpu.SemaphoreType.DMA((height // step,))],
        compiler_params=params(4 * MIB),
        cost_estimate=cost(0, 2 * height * units),
        name="patch",
    )(*in_smem(kept, *lists), *in_vmem(delta), *in_hbm(weight))


def moment_copies(which, sources, targets, sems, row=0):
    return [
        pltpu.make_async_copy(source.at[which], target, sems.at[i, row])
        for i, (source, target) in enumerate(zip(sources, targets))
    ]


def moments_kernel(which, first, second, first_out, second_out, sems):
    copies = moment_copies(which, (first, second), (first_out, second_out), sems)
    for copy in copies:
        copy.start()
    for copy in copies:
        copy.wait()


def moments(which, first, second):
    out = pltpu.VMEM(first.shape[1:], F32)
    return pl.pallas_call(
        functools.partial(moments_kernel, which),
        out_shape=(out, out),
        in_specs=[HBM_SPEC] * 2,
        scratch_shapes=[pltpu.SemaphoreType.DMA((2, 1))],
        compiler_params=params(2 * MIB),
        cost_estimate=cost(0, 8 * first[0].size),
        name="moments",
    )(*in_hbm(first, second))


def layer_kernel(
    wide, step, kept, counts, begins, entries, tokens_0, tokens_1, cotangent_0, cotangent_1,
    gate_0, gate_1, up_delta, down_delta, up_weight, down_weight, first, second,
    keep, send, tokens, cotangent, hidden, gate_grad, up_grad, *refs,
):
    moments_out = refs[:-7]
    up_eff, ring, gate, up, ring_sems, part_sems, moment_sems = refs[-7:]
    width, units = up_eff.shape
    tiles, slots, side = up_delta.shape[:3]
    half = keep.shape[0]
    depth, height, span = ring.shape
    across = width // span
    chunks = (units // height) * across

    def down_copy(c):
        source = down_weight.at[chunk(c // across, height), chunk(c % across, span)]
        return pltpu.make_async_copy(source, ring.at[c % depth], ring_sems.at[c % depth])

    lower = width // 2
    parts = width // wide
    flight = 3

    def part_copy(p):
        rows = chunk(p, wide)
        return pltpu.make_async_copy(up_weight.at[rows], up_eff.at[rows], part_sems.at[p])

    def start(j):
        @pl.when(j < parts)
        def _():
            part_copy(j).start()

        @pl.when((j >= parts) & (j < parts + min(depth, chunks)))
        def _():
            down_copy(j - parts).start()

    for j in range(flight):
        start(j)
    for whole, part_0, part_1 in (
        (tokens, tokens_0, tokens_1),
        (cotangent, cotangent_0, cotangent_1),
    ):
        whole[:half] = part_0[...]
        whole[half:] = part_1[...]
    gate[...] = jnp.zeros_like(gate)
    up[...] = jnp.zeros_like(up)

    def product(out, eff, first_part, i):
        left = tokens[:, chunk(first_part + i, wide)]
        out[...] += jnp.dot(left, eff[chunk(i, wide), :], preferred_element_type=F32)

    def forward_gate(eff, first_part, i, carry):
        product(gate, eff, first_part, i)
        return carry

    def forward_up(p, carry):
        part_copy(p).wait()
        start(p + flight)
        span = wide * PARTS // width
        add_column_blocks(1, kept, begins, entries, up_delta, up_eff, 0, p * span, span)
        product(up, up_eff, 0, p)
        return carry

    lax.fori_loop(0, parts // 2, functools.partial(forward_gate, gate_0, 0), 0)
    lax.fori_loop(0, parts // 2, functools.partial(forward_gate, gate_1, parts // 2), 0)
    lax.fori_loop(0, parts, forward_up, 0)

    def backward(r, carry):
        hidden_grad = jnp.zeros((2 * half, height), F32)
        for q in range(across):
            c = r * across + q
            down_copy(c).wait()
            slot = ring.at[c % depth]
            for i in range(height // side):
                t = r * (height // side) + i
                for k in range(slots):
                    col = kept[2, k, t] * side - q * span

                    @pl.when((k < counts[2, t]) & (col >= 0) & (col < span))
                    def _():
                        cols = pl.ds(pl.multiple_of(col, side), side)
                        add_block(slot, slice(i * side, (i + 1) * side), cols, down_delta[t, k])

            hidden_grad += dot_rows(cotangent[:, q * span : (q + 1) * span], slot[...])

            @pl.when(c + depth < chunks)
            def _():
                down_copy(c + depth).start()

        own = chunk(r, height)
        g, u = gate[:, own], up[:, own]
        sigma = jax.nn.sigmoid(g)
        silu = g * sigma
        hidden[:, own] = (silu * u).astype(BF16)
        gate_grad[:, own] = (hidden_grad * u * sigma * (1.0 + g * (1.0 - sigma))).astype(BF16)
        up_grad[:, own] = (hidden_grad * silu).astype(BF16)
        return carry

    lax.fori_loop(0, units // height, backward, 0)
    copies = []
    for which in range(len(moments_out) // 2):
        targets = moments_out[2 * which : 2 * which + 2]
        copies += moment_copies(which, (first, second), targets, moment_sems, which)
    for copy in copies:
        copy.start()

    def input_part(gate_eff, offset, i, carry):
        cols = chunk(offset // step + i, step)
        both = dot_rows(gate_eff[chunk(i, step), :], gate_grad[...])
        both = (both + dot_rows(up_eff[cols, :], up_grad[...])).T
        keep[:, cols] = both[:half]
        send[:, cols] = both[half:].astype(BF16)
        return carry

    lax.fori_loop(0, lower // step, functools.partial(input_part, gate_0, 0), 0)
    lax.fori_loop(0, lower // step, functools.partial(input_part, gate_1, lower), 0)
    for copy in copies:
        copy.wait()


def layer(ahead, kept, counts, lists, tokens, cotangent, gate_eff, deltas, up_weight, down_weight, first, second):
    rows, width = 2 * tokens[0].shape[0], tokens[0].shape[1]
    units = gate_eff[0].shape[1]
    shape = first.shape
    tiles, side = shape[1], shape[-1]
    height, span = min(2, tiles) * side, width // 2
    wide, step = width // 4, width // 4
    grad = pltpu.VMEM((rows, units), BF16)
    return pl.pallas_call(
        functools.partial(layer_kernel, wide, step),
        out_shape=(
            pltpu.VMEM((rows // 2, width), F32),
            pltpu.VMEM((rows // 2, width), BF16),
            pltpu.VMEM((rows, width), BF16),
            pltpu.VMEM((rows, width), BF16),
            grad,
            grad,
            grad,
            *(pltpu.VMEM(shape[1:], F32),) * (2 * ahead),
        ),
        in_specs=[SMEM_SPEC] * 4 + [VMEM_SPEC] * 8 + [HBM_SPEC] * 4,
        scratch_shapes=[
            pltpu.VMEM((width, units), BF16),
            pltpu.VMEM((3, height, span), BF16),
            pltpu.VMEM((rows, units), F32),
            pltpu.VMEM((rows, units), F32),
            pltpu.SemaphoreType.DMA((3,)),
            pltpu.SemaphoreType.DMA((width // wide,)),
            pltpu.SemaphoreType.DMA((2, max(ahead, 1))),
        ],
        compiler_params=params(25 * MIB),
        cost_estimate=cost(10 * rows * width * units, 10 * width * units),
        name="layer",
    )(
        *in_smem(kept, counts, *lists),
        *in_vmem(*tokens, *cotangent, *gate_eff, *deltas[1:]),
        *in_hbm(up_weight, down_weight, first, second),
    )


def adam_kernel(which, kept, counts, left, right, delta, first, second, *refs):
    outs = refs[-5:-2]
    made, sems = refs[-2:]
    tiles, slots, side = delta.shape[:3]

    def write(a, t):
        return pltpu.make_async_copy(made.at[a, t], outs[a].at[which, t], sems.at[a, t])

    def tile(t, carry):
        own = chunk(t, side)
        for k in range(slots):
            block = chunk(kept[which, k, t], side)
            if which == 2:
                grad = dot_cols(left[:, own], right[:, block])
            else:
                grad = dot_cols(left[:, block], right[:, own])
            live = k < counts[which, t]
            m1 = 0.9 * first[t, k] + 0.1 * grad
            m2 = 0.999 * second[t, k] + 0.001 * grad * grad
            value = delta[t, k] - 0.01 * m1 / (jnp.sqrt(m2) + 1e-08)
            for a, new in enumerate((value, m1, m2)):
                made[a, t, k] = jnp.where(live, new, 0.0)
        for a in range(3):
            write(a, t).start()
        return carry

    lax.fori_loop(0, tiles, tile, 0, unroll=min(tiles, 4))
    for t in range(tiles):
        for a in range(3):
            write(a, t).wait()


def adam(which, kept, counts, left, right, delta, moment_pair, done):
    shape = (3, *delta.shape)
    out = pltpu.HBM(shape, F32)
    return pl.pallas_call(
        functools.partial(adam_kernel, which),
        out_shape=(out, out, out),
        in_specs=[SMEM_SPEC] * 2 + [VMEM_SPEC] * 5 + [HBM_SPEC] * len(done),
        out_specs=(HBM_SPEC,) * 3,
        scratch_shapes=[pltpu.VMEM((3, *shape[1:]), F32), pltpu.SemaphoreType.DMA((3, shape[1]))],
        input_output_aliases={7 + i: i for i in range(len(done))},
        compiler_params=params(8 * MIB),
        cost_estimate=cost(0, 12 * delta.size),
        name="adam",
    )(*in_smem(kept, counts), *in_vmem(left, right, delta, *moment_pair), *in_hbm(*done))


def exchange(value, distance, size):
    return lax.ppermute(value, "dp", [(i, i ^ distance) for i in range(size)])


def exchange_order(size):
    distances = [1 << bit for bit in range(size.bit_length() - 1)]
    return distances[::-1], distances[1:2] + distances[:1:-1] + distances[:1]


def joined(own, got, early):
    if not early:
        return jnp.concatenate([own, got], 0)
    half = own.shape[0] // 2
    return jnp.concatenate([own[:half], got[:half], own[half:], got[half:]], 0)


def after(value, *others):
    return lax.optimization_barrier((value, others))[0]


def on_device(
    size,
    tokens,
    cotangent,
    gate_weight,
    up_weight,
    down_weight,
    kept_blocks,
    kept_counts,
    sparse_delta,
    first_moment,
    second_moment,
):
    order, other_order = exchange_order(size)
    raw = (tokens, cotangent)
    tokens, cotangent, kept, counts, *deltas, begins, entries = into_vmem(
        tokens, cotangent, kept_blocks.transpose(0, 2, 1), kept_counts, sparse_delta
    )
    half = gate_weight.shape[0] // 2
    lists = (begins, entries)
    pair = (tokens, cotangent)
    gate_eff = []
    for i, distances in enumerate(zip(order, other_order)):
        sent = pair if i else raw
        got = tuple(exchange(rows, distance, size) for rows, distance in zip(sent, distances))
        if max(len(order) - 3, 0) <= i < len(order) - 1:
            offset = len(gate_eff) * half
            gate_eff.append(patched(0, offset, half, after(kept, *pair), lists, deltas[0], gate_weight))
        if i < len(order) - 1:
            pair = (joined(pair[0], got[0], False), joined(pair[1], got[1], i > 0))
            pair = after(pair, *deltas, *lists, *gate_eff[-1:])
    tokens, cotangent = zip(pair, got)
    ahead = 3
    total, away, tokens, cotangent, hidden, gate_grad, up_grad, *fetched = layer(
        ahead, kept, counts, lists, tokens, cotangent, gate_eff, deltas, up_weight, down_weight, first_moment, second_moment
    )
    operands = ((tokens, gate_grad), (tokens, up_grad), (hidden, cotangent))
    news = ()
    for i, distance in enumerate(order[::-1]):
        if i:
            half = total.shape[0] // 2
            total, away = total[:half], total[half:].astype(BF16)
        got = exchange(away, distance, size)
        which = i - (len(order) - 3)
        if which == -1 or (which == 0 and i == 0):
            for late in range(ahead, 3):
                fetched += moments(late, after(first_moment, away), second_moment)
            got = after(got, *fetched)
        if which >= 0:
            pair = fetched[2 * which : 2 * which + 2]
            news = adam(which, after(kept, away), counts, *operands[which], deltas[which], pair, news)
        total = total + got.astype(F32)
        if which >= 0:
            total = after(total, *news)
    return (total.astype(BF16), *news)


def solution(mesh):
    rows = P(("groups", "dp"), None)
    blocks = P("groups", "dp", None, None, None)
    return jax.shard_map(
        functools.partial(on_device, mesh.shape["dp"]),
        mesh=mesh,
        in_specs=(
            rows,
            rows,
            P(None, "dp"),
            P(None, "dp"),
            P("dp", None),
            P("groups", "dp", None),
            P("groups", "dp"),
            blocks,
            blocks,
            blocks,
        ),
        out_specs=(rows, blocks, blocks, blocks),
        check_vma=False,
    )
```

```python
import functools

import jax
import jax.numpy as jnp
from jax import lax
from jax.experimental import pallas as pl
from jax.experimental.pallas import tpu as pltpu
from jax.sharding import PartitionSpec as P

BF16 = jnp.bfloat16
F32 = jnp.float32
MIB = 1 << 20
VMEM_SPEC = pl.BlockSpec(memory_space=pltpu.VMEM)
SMEM_SPEC = pl.BlockSpec(memory_space=pltpu.SMEM)
HBM_SPEC = pl.BlockSpec(memory_space=pltpu.HBM)


def in_hbm(*arrays):
    return [pltpu.with_memory_space_constraint(array, pltpu.HBM) for array in arrays]


def in_vmem(*arrays):
    return [pltpu.with_memory_space_constraint(array, pltpu.VMEM) for array in arrays]


def in_smem(*arrays):
    return [pltpu.with_memory_space_constraint(array, pltpu.SMEM) for array in arrays]


def dot_rows(left, right):
    return lax.dot_general(left, right, (((1,), (1,)), ((), ())), preferred_element_type=F32)


def dot_cols(left, right):
    return lax.dot_general(left, right, (((0,), (0,)), ((), ())), preferred_element_type=F32)


def chunk(i, size):
    return pl.ds(pl.multiple_of(i * size, size), size)


def params(limit):
    return pltpu.CompilerParams(vmem_limit_bytes=limit)


def cost(flops, moved):
    return pl.CostEstimate(flops=flops, bytes_accessed=moved, transcendentals=0)


def add_block(ref, rows, cols, block):
    ref[rows, cols] = (ref[rows, cols].astype(F32) + block).astype(BF16)


PARTS = 8


def list_live(per_part, kept, counts, begins, entries):
    _, slots, tiles = kept.shape
    for m in range(entries.shape[0]):

        def each(step, m=m):
            def tile(t, carry):
                for k in range(slots):

                    @pl.when(k < counts[m, t])
                    def _():
                        step(lax.div(kept[m, k, t], per_part), t * slots + k)

                return carry

            lax.fori_loop(0, tiles, tile, 0)

        def count(part, entry, m=m):
            begins[m, part + 1] += 1

        def place(part, entry, m=m):
            at = begins[m, part]
            entries[m, at] = entry
            begins[m, part] = at + 1

        for part in range(PARTS + 1):
            begins[m, part] = 0
        each(count)
        for part in range(PARTS):
            begins[m, part + 1] += begins[m, part]
        each(place)
        for part in range(PARTS, 0, -1):
            begins[m, part] = begins[m, part - 1]
        begins[m, 0] = 0


def enter_kernel(per_part, count, *refs):
    blocks, targets, sems = refs[count], refs[count + 1 : -3], refs[-1]
    begins, entries = refs[-3:-1]
    sources = [*refs[:count], *(blocks.at[i] for i in range(blocks.shape[0]))]
    copies = [
        pltpu.make_async_copy(source, target, sems.at[i])
        for i, (source, target) in enumerate(zip(sources, targets))
    ]
    for copy in copies:
        copy.start()
    for copy in copies[:count]:
        copy.wait()
    list_live(per_part, targets[count - 2], targets[count - 1], begins, entries)
    for copy in copies[count:]:
        copy.wait()


def into_vmem(*arrays):
    *whole, blocks = arrays
    _, tiles, slots, side, _ = blocks.shape
    shapes = [array.shape for array in whole] + [blocks.shape[1:]] * blocks.shape[0]
    kinds = [array.dtype for array in whole] + [blocks.dtype] * blocks.shape[0]
    shapes += [(2, PARTS + 1), (2, tiles * slots)]
    kinds += [jnp.int32] * 2
    per_part = whole[0].shape[1] // (PARTS * side)
    return pl.pallas_call(
        functools.partial(enter_kernel, per_part, len(whole)),
        out_shape=tuple(
            (pltpu.SMEM if kind == jnp.int32 else pltpu.VMEM)(shape, kind)
            for shape, kind in zip(shapes, kinds)
        ),
        out_specs=tuple(SMEM_SPEC if kind == jnp.int32 else VMEM_SPEC for kind in kinds),
        in_specs=[HBM_SPEC] * len(arrays),
        scratch_shapes=[pltpu.SemaphoreType.DMA((len(shapes) - 2,))],
        compiler_params=params(2 * MIB),
        name="enter",
    )(*in_hbm(*arrays))


def add_column_blocks(which, kept, begins, entries, delta, ref, offset, part, span):
    slots, side = delta.shape[1:3]

    def add(i, carry):
        entry = entries[which, i]
        t, k = lax.div(entry, slots), lax.rem(entry, slots)
        row = kept[which, k, t] * side - offset
        add_block(ref, pl.ds(pl.multiple_of(row, side), side), chunk(t, side), delta[t, k])
        return carry

    lax.fori_loop(begins[which, part], begins[which, part + span], add, 0)


def patch_kernel(which, offset, step, kept, begins, entries, delta, weight, out, sems):
    parts = out.shape[0] // step

    def part_copy(p):
        source = weight.at[pl.ds(offset + p * step, step)]
        return pltpu.make_async_copy(source, out.at[pl.ds(p * step, step)], sems.at[p])

    for p in range(parts):
        part_copy(p).start()
    for p in range(parts):
        part_copy(p).wait()
        add_column_blocks(which, kept, begins, entries, delta, out, offset, offset // step + p, 1)


def patched(which, offset, height, kept, lists, delta, weight):
    units = weight.shape[1]
    step = weight.shape[0] // PARTS
    return pl.pallas_call(
        functools.partial(patch_kernel, which, offset, step),
        out_shape=pltpu.VMEM((height, units), BF16),
        in_specs=[SMEM_SPEC] * 3 + [VMEM_SPEC, HBM_SPEC],
        scratch_shapes=[pltpu.SemaphoreType.DMA((height // step,))],
        compiler_params=params(4 * MIB),
        cost_estimate=cost(0, 2 * height * units),
        name="patch",
    )(*in_smem(kept, *lists), *in_vmem(delta), *in_hbm(weight))


def moment_copies(which, sources, targets, sems, row=0):
    return [
        pltpu.make_async_copy(source.at[which], target, sems.at[i, row])
        for i, (source, target) in enumerate(zip(sources, targets))
    ]


def moments_kernel(which, first, second, first_out, second_out, sems):
    copies = moment_copies(which, (first, second), (first_out, second_out), sems)
    for copy in copies:
        copy.start()
    for copy in copies:
        copy.wait()


def moments(which, first, second):
    out = pltpu.VMEM(first.shape[1:], F32)
    return pl.pallas_call(
        functools.partial(moments_kernel, which),
        out_shape=(out, out),
        in_specs=[HBM_SPEC] * 2,
        scratch_shapes=[pltpu.SemaphoreType.DMA((2, 1))],
        compiler_params=params(2 * MIB),
        cost_estimate=cost(0, 8 * first[0].size),
        name="moments",
    )(*in_hbm(first, second))


def layer_kernel(
    wide, step, kept, counts, begins, entries, tokens_0, tokens_1, cotangent_0, cotangent_1,
    gate_0, gate_1, up_delta, down_delta, up_weight, down_weight, first, second,
    keep, send, tokens, cotangent, hidden, gate_grad, up_grad, *refs,
):
    moments_out = refs[:-7]
    up_eff, ring, gate, up, ring_sems, part_sems, moment_sems = refs[-7:]
    width, units = up_eff.shape
    tiles, slots, side = up_delta.shape[:3]
    half = keep.shape[0]
    depth, height, span = ring.shape
    across = width // span
    chunks = (units // height) * across

    def down_copy(c):
        source = down_weight.at[chunk(c // across, height), chunk(c % across, span)]
        return pltpu.make_async_copy(source, ring.at[c % depth], ring_sems.at[c % depth])

    lower = width // 2
    parts = width // wide
    flight = 3

    def part_copy(p):
        rows = chunk(p, wide)
        return pltpu.make_async_copy(up_weight.at[rows], up_eff.at[rows], part_sems.at[p])

    def start(j):
        @pl.when(j < parts)
        def _():
            part_copy(j).start()

        @pl.when((j >= parts) & (j < parts + min(depth, chunks)))
        def _():
            down_copy(j - parts).start()

    for j in range(flight):
        start(j)
    for whole, part_0, part_1 in (
        (tokens, tokens_0, tokens_1),
        (cotangent, cotangent_0, cotangent_1),
    ):
        whole[:half] = part_0[...]
        whole[half:] = part_1[...]
    gate[...] = jnp.zeros_like(gate)
    up[...] = jnp.zeros_like(up)

    def product(out, eff, first_part, i):
        left = tokens[:, chunk(first_part + i, wide)]
        out[...] += jnp.dot(left, eff[chunk(i, wide), :], preferred_element_type=F32)

    def forward_gate(eff, first_part, i, carry):
        product(gate, eff, first_part, i)
        return carry

    def forward_up(p, carry):
        part_copy(p).wait()
        start(p + flight)
        span = wide * PARTS // width
        add_column_blocks(1, kept, begins, entries, up_delta, up_eff, 0, p * span, span)
        product(up, up_eff, 0, p)
        return carry

    lax.fori_loop(0, parts // 2, functools.partial(forward_gate, gate_0, 0), 0)
    lax.fori_loop(0, parts // 2, functools.partial(forward_gate, gate_1, parts // 2), 0)
    lax.fori_loop(0, parts, forward_up, 0)

    def backward(r, carry):
        hidden_grad = jnp.zeros((2 * half, height), F32)
        for q in range(across):
            c = r * across + q
            down_copy(c).wait()
            slot = ring.at[c % depth]
            for i in range(height // side):
                t = r * (height // side) + i
                for k in range(slots):
                    col = kept[2, k, t] * side - q * span

                    @pl.when((k < counts[2, t]) & (col >= 0) & (col < span))
                    def _():
                        cols = pl.ds(pl.multiple_of(col, side), side)
                        add_block(slot, slice(i * side, (i + 1) * side), cols, down_delta[t, k])

            hidden_grad += dot_rows(cotangent[:, q * span : (q + 1) * span], slot[...])

            @pl.when(c + depth < chunks)
            def _():
                down_copy(c + depth).start()

        own = chunk(r, height)
        g, u = gate[:, own], up[:, own]
        sigma = jax.nn.sigmoid(g)
        silu = g * sigma
        hidden[:, own] = (silu * u).astype(BF16)
        gate_grad[:, own] = (hidden_grad * u * sigma * (1.0 + g * (1.0 - sigma))).astype(BF16)
        up_grad[:, own] = (hidden_grad * silu).astype(BF16)
        return carry

    lax.fori_loop(0, units // height, backward, 0)
    copies = []
    for which in range(len(moments_out) // 2):
        targets = moments_out[2 * which : 2 * which + 2]
        copies += moment_copies(which, (first, second), targets, moment_sems, which)
    for copy in copies:
        copy.start()

    def input_part(gate_eff, offset, i, carry):
        cols = chunk(offset // step + i, step)
        both = dot_rows(gate_eff[chunk(i, step), :], gate_grad[...])
        both = (both + dot_rows(up_eff[cols, :], up_grad[...])).T
        keep[:, cols] = both[:half]
        send[:, cols] = both[half:].astype(BF16)
        return carry

    lax.fori_loop(0, lower // step, functools.partial(input_part, gate_0, 0), 0)
    lax.fori_loop(0, lower // step, functools.partial(input_part, gate_1, lower), 0)
    for copy in copies:
        copy.wait()


def layer(ahead, kept, counts, lists, tokens, cotangent, gate_eff, deltas, up_weight, down_weight, first, second):
    rows, width = 2 * tokens[0].shape[0], tokens[0].shape[1]
    units = gate_eff[0].shape[1]
    shape = first.shape
    tiles, side = shape[1], shape[-1]
    height, span = min(2, tiles) * side, width // 2
    wide, step = width // 4, width // 4
    grad = pltpu.VMEM((rows, units), BF16)
    return pl.pallas_call(
        functools.partial(layer_kernel, wide, step),
        out_shape=(
            pltpu.VMEM((rows // 2, width), F32),
            pltpu.VMEM((rows // 2, width), BF16),
            pltpu.VMEM((rows, width), BF16),
            pltpu.VMEM((rows, width), BF16),
            grad,
            grad,
            grad,
            *(pltpu.VMEM(shape[1:], F32),) * (2 * ahead),
        ),
        in_specs=[SMEM_SPEC] * 4 + [VMEM_SPEC] * 8 + [HBM_SPEC] * 4,
        scratch_shapes=[
            pltpu.VMEM((width, units), BF16),
            pltpu.VMEM((3, height, span), BF16),
            pltpu.VMEM((rows, units), F32),
            pltpu.VMEM((rows, units), F32),
            pltpu.SemaphoreType.DMA((3,)),
            pltpu.SemaphoreType.DMA((width // wide,)),
            pltpu.SemaphoreType.DMA((2, max(ahead, 1))),
        ],
        compiler_params=params(25 * MIB),
        cost_estimate=cost(10 * rows * width * units, 10 * width * units),
        name="layer",
    )(
        *in_smem(kept, counts, *lists),
        *in_vmem(*tokens, *cotangent, *gate_eff, *deltas[1:]),
        *in_hbm(up_weight, down_weight, first, second),
    )


def adam_kernel(ranges, kept, counts, hidden, gate_grad, up_grad, tokens, cotangent, *refs):
    used = len({which for which, _, _ in ranges})
    deltas, firsts, seconds = refs[:used], refs[used : 2 * used], refs[2 * used : 3 * used]
    outs = refs[-5:-2]
    made, sems = refs[-2:]
    slots, side = made.shape[2:4]
    order = []

    for i, (which, begin, end) in enumerate(ranges):
        delta, first, second = deltas[i], firsts[i], seconds[i]
        base = len(order)

        def write(a, t, place, which=which):
            return pltpu.make_async_copy(made.at[a, place], outs[a].at[which, t], sems.at[a, place])

        def tile(t, carry):
            place = base + t - begin
            own = chunk(t, side)
            for k in range(slots):
                block = chunk(kept[which, k, t], side)
                if which == 2:
                    grad = dot_cols(hidden[:, own], cotangent[:, block])
                else:
                    grad = dot_cols(tokens[:, block], (gate_grad, up_grad)[which][:, own])
                live = k < counts[which, t]
                m1 = 0.9 * first[t, k] + 0.1 * grad
                m2 = 0.999 * second[t, k] + 0.001 * grad * grad
                value = delta[t, k] - 0.01 * m1 / (jnp.sqrt(m2) + 1e-08)
                for a, new in enumerate((value, m1, m2)):
                    made[a, place, k] = jnp.where(live, new, 0.0)
            for a in range(3):
                write(a, t, place).start()
            return carry

        count = end - begin
        lax.fori_loop(begin, end, tile, 0, unroll=4 if count % 4 == 0 else 2 if count % 2 == 0 else 1)
        order += [(write, t, base + t - begin) for t in range(begin, end)]
    for write, t, place in order:
        for a in range(3):
            write(a, t, place).wait()


def adam(ranges, kept, counts, operands, deltas, fetched, done):
    blocks = deltas[0].shape
    tiles = sum(end - begin for _, begin, end in ranges)
    inputs = [
        *operands,
        *(deltas[which] for which, _, _ in ranges),
        *(fetched[2 * which] for which, _, _ in ranges),
        *(fetched[2 * which + 1] for which, _, _ in ranges),
    ]
    out = pltpu.HBM((3, *blocks), F32)
    return pl.pallas_call(
        functools.partial(adam_kernel, ranges),
        out_shape=(out, out, out),
        in_specs=[SMEM_SPEC] * 2 + [VMEM_SPEC] * len(inputs) + [HBM_SPEC] * len(done),
        out_specs=(HBM_SPEC,) * 3,
        scratch_shapes=[pltpu.VMEM((3, tiles, *blocks[1:]), F32), pltpu.SemaphoreType.DMA((3, tiles))],
        input_output_aliases={2 + len(inputs) + i: i for i in range(len(done))},
        compiler_params=params(11 * MIB),
        cost_estimate=cost(0, 12 * tiles * deltas[0][0].size),
        name="adam",
    )(*in_smem(kept, counts), *in_vmem(*inputs), *in_hbm(*done))


def adam_pieces(tiles):
    cut = tiles // 4
    pieces = (
        ((2, 0, cut),),
        ((0, 0, tiles), (1, 0, cut)),
        ((1, cut, tiles),),
        ((2, cut, tiles),),
    )
    return [tuple(r for r in ranges if r[1] < r[2]) for ranges in pieces]


def exchange(value, distance, size):
    return lax.ppermute(value, "dp", [(i, i ^ distance) for i in range(size)])


def exchange_order(size):
    distances = [1 << bit for bit in range(size.bit_length() - 1)]
    return distances[::-1], distances[1:2] + distances[:1:-1] + distances[:1]


def joined(own, got, early):
    if not early:
        return jnp.concatenate([own, got], 0)
    half = own.shape[0] // 2
    return jnp.concatenate([own[:half], got[:half], own[half:], got[half:]], 0)


def after(value, *others):
    return lax.optimization_barrier((value, others))[0]


def on_device(
    size,
    tokens,
    cotangent,
    gate_weight,
    up_weight,
    down_weight,
    kept_blocks,
    kept_counts,
    sparse_delta,
    first_moment,
    second_moment,
):
    order, other_order = exchange_order(size)
    raw = (tokens, cotangent)
    tokens, cotangent, kept, counts, *deltas, begins, entries = into_vmem(
        tokens, cotangent, kept_blocks.transpose(0, 2, 1), kept_counts, sparse_delta
    )
    half = gate_weight.shape[0] // 2
    lists = (begins, entries)
    pair = (tokens, cotangent)
    gate_eff = []
    for i, distances in enumerate(zip(order, other_order)):
        sent = pair if i else raw
        got = tuple(exchange(rows, distance, size) for rows, distance in zip(sent, distances))
        if max(len(order) - 3, 0) <= i < len(order) - 1:
            offset = len(gate_eff) * half
            gate_eff.append(patched(0, offset, half, after(kept, *pair), lists, deltas[0], gate_weight))
        if i < len(order) - 1:
            pair = (joined(pair[0], got[0], False), joined(pair[1], got[1], i > 0))
            pair = after(pair, *deltas, *lists, *gate_eff[-1:])
    tokens, cotangent = zip(pair, got)
    ahead = 3
    total, away, tokens, cotangent, hidden, gate_grad, up_grad, *fetched = layer(
        ahead, kept, counts, lists, tokens, cotangent, gate_eff, deltas, up_weight, down_weight, first_moment, second_moment
    )
    operands = (hidden, gate_grad, up_grad, tokens, cotangent)
    pieces = adam_pieces(sparse_delta.shape[1])
    news = ()
    for i, distance in enumerate(order[::-1]):
        if i:
            half = total.shape[0] // 2
            total, away = total[:half], total[half:].astype(BF16)
        got = exchange(away, distance, size)
        piece = i - (len(order) - 4)
        ranges = pieces[piece] if piece >= 0 else ()
        if ranges:
            news = adam(ranges, after(kept, away), counts, operands, deltas, fetched, news)
        total = total + got.astype(F32)
        if ranges:
            total = after(total, *news)
    return (total.astype(BF16), *news)


def solution(mesh):
    rows = P(("groups", "dp"), None)
    blocks = P("groups", "dp", None, None, None)
    return jax.shard_map(
        functools.partial(on_device, mesh.shape["dp"]),
        mesh=mesh,
        in_specs=(
            rows,
            rows,
            P(None, "dp"),
            P(None, "dp"),
            P("dp", None),
            P("groups", "dp", None),
            P("groups", "dp"),
            blocks,
            blocks,
            blocks,
        ),
        out_specs=(rows, blocks, blocks, blocks),
        check_vma=False,
    )
```
